1024 devices in a mesh: gx: 4 (over y_lo, core), gy: 4 (over y_hi), gz: 64 (over z, x).
Axes of the slice: x: 8, y: 8 (y_hi: 4, y_lo: 2; y = y_hi * 2 + y_lo), z: 8, core: 2. Of those that a mesh axis runs over, the one named last changes fastest.
Arguments:
- offsets: float32 [3, 4, 8, 128, 128], P(None, 'gx', 'gy', 'gz'), may hold values from 0 to 11, as said below
- type_ids: int32 [4, 8, 128, 128], P('gx', 'gy', 'gz'), may hold values from 0 to 1
- neighbours: int32 [4, 8, 128, 27], P('gx', 'gy', 'gz'), may hold values from 0 to 48, as said below
- type_chi: float32 [2], replicated, may hold values from 3 to 7
- type_eta: float32 [2], replicated, may hold values from 6 to 12
- type_gamma: float32 [2], replicated, may hold values from 0.5 to 1
Outputs:
- charges: float32 [4, 8, 128, 128], P('gx', 'gy', 'gz')
- residuals: float32 [2, 4, 8, 128, 128], P(None, 'gx', 'gy', 'gz')
The draws below stay inside these ranges and needn't reach their ends.
Inputs may be any that keep to these rules, and one draw needn't show every extreme that they name: `neighbours`: each tile's row lists the tile itself and some of the 26 cells around it, each at most once, as indices into its device's block padded by one cell on every side (3) x (4) x (4) in first-dimension-major order; unused slots hold (3) * 4 * 4. Two tiles list each other with opposite displacements or not at all. `offsets`: any two atoms of the box lie at least 0.8 A apart.
All inputs are finite; a program needn't handle non-finite values.
Results may differ from the reference program's by a relative error of at most 0.0003.
Values sent between devices are 32-bit elements; how exact they have to be, the bound alone decides.
No kernel may reach another device: no remote copies, remote signals or barrier semaphores. Data moves between devices by JAX's collectives and lax.ppermute only.
A program may use at most 32 MiB of HBM per device.

```python
import jax
import jax.numpy as jnp
import numpy as np
from jax import lax

ATOMS = 128
NB = 27
TYPES = 2
ITERS = 3
CX = 1
CY = 2
CZ = 2
NCX = 4
NCY = 8
NCZ = 128


def lattice_sites():
    side = 1
    while (side + 1) ** 3 <= ATOMS:
        side = side + 1
    spacing = 11.0 / side
    points = []
    for first_step in range(side):
        for second_step in range(side):
            for third_step in range(side):
                points.append([(first_step + 0.5) * spacing, (second_step + 0.5) * spacing, (third_step + 0.5) * spacing])
    inner = max(side - 1, 1)
    extra_count = ATOMS - side ** 3
    for extra_index in range(extra_count):
        first_step = extra_index // (inner * inner)
        second_step = extra_index // inner % inner
        third_step = extra_index % inner
        points.append([spacing, spacing, (third_step + 1.0) * spacing])
    return np.array(points, dtype=np.float32).T


def draw_offsets(key, part):
    base = jnp.asarray(lattice_sites())[:, None, None, None, :]
    jitter = jnp.clip(0.12 * jax.random.normal(key, (3, NCX, NCY, NCZ, ATOMS), jnp.float32), -0.3, 0.3)
    return jnp.clip(base + jitter, 0.0, 10.999).astype(jnp.float32)


def draw_neighbours(key, part):
    offset_table = np.array([[first_step, second_step, third_step] for first_step in (-1, 0, 1) for second_step in (-1, 0, 1) for third_step in (-1, 0, 1)], dtype=np.int32)
    keep_bits = jax.random.randint(key, (NCX, NCY, NCZ, 13), 0, 4) > 0
    columns = []
    for slot_index in range(27):
        if slot_index < 13:
            columns.append(keep_bits[..., slot_index])
        elif slot_index == 13:
            columns.append(jnp.ones((NCX, NCY, NCZ), dtype=bool))
        else:
            mirror = 26 - slot_index
            moved = offset_table[slot_index]
            columns.append(jnp.roll(keep_bits[..., mirror], shift=(-int(moved[0]), -int(moved[1]), -int(moved[2])), axis=(0, 1, 2)))
    kept = jnp.stack(columns, -1)
    local_one = (jnp.arange(NCX, dtype=jnp.int32) % CX)[:, None, None, None]
    local_two = (jnp.arange(NCY, dtype=jnp.int32) % CY)[None, :, None, None]
    local_three = (jnp.arange(NCZ, dtype=jnp.int32) % CZ)[None, None, :, None]
    table_one = jnp.asarray(offset_table[:, 0])[None, None, None, :]
    table_two = jnp.asarray(offset_table[:, 1])[None, None, None, :]
    table_three = jnp.asarray(offset_table[:, 2])[None, None, None, :]
    padded_index = ((local_one + 1 + table_one) * (CY + 2) + (local_two + 1 + table_two)) * (CZ + 2) + (local_three + 1 + table_three)
    padded_index = jnp.broadcast_to(padded_index, (NCX, NCY, NCZ, 27))
    sentinel = (CX + 2) * (CY + 2) * (CZ + 2)
    slot_order = jnp.arange(27, dtype=jnp.int32)[None, None, None, :]
    order_key = jnp.where(kept, slot_order, slot_order + 27)
    order = jnp.argsort(order_key, axis=-1, stable=True)
    index_sorted = jnp.take_along_axis(padded_index, order, -1)
    kept_sorted = jnp.take_along_axis(kept, order, -1)
    return jnp.where(kept_sorted, index_sorted, sentinel).astype(jnp.int32)


def touch_ends(values, stream_key, least, top_value):
    shape = values.shape
    spot = [jax.random.randint(jax.random.fold_in(stream_key, axis), (), 0, shape[axis]) for axis in range(len(shape))]
    values = values.at[tuple(spot)].set(least)
    longest = shape.index(max(shape))
    spot[longest] = (spot[longest] + 1) % shape[longest]
    return values.at[tuple(spot)].set(top_value)


def setup_inputs(seed: int = 0) -> dict:
    arg_keys = jax.random.split(jax.random.key(seed), 7)
    return {
        "offsets": draw_offsets(jax.random.fold_in(arg_keys[6], 71), 0),
        "type_ids": touch_ends(jax.random.randint(arg_keys[1], (NCX, NCY, NCZ, ATOMS), 0, TYPES), jax.random.fold_in(arg_keys[1], 1), 0, TYPES - 1).astype(jnp.int32),
        "neighbours": draw_neighbours(jax.random.fold_in(arg_keys[6], 71), 0),
        "type_chi": jnp.clip(jax.random.uniform(arg_keys[3], (TYPES,), jnp.float32, 3.0, 7.0), 3.0, 7.0),
        "type_eta": jnp.clip(jax.random.uniform(arg_keys[4], (TYPES,), jnp.float32, 6.0, 12.0), 6.0, 12.0),
        "type_gamma": jnp.clip(jax.random.uniform(arg_keys[5], (TYPES,), jnp.float32, 0.5, 1.0), 0.5, 1.0),
    }


CELL_EDGE = 11.0
CUTOFF = 10.0
COULOMB = 14.4

def taper_value(distance):
    scaled = distance / CUTOFF
    squared = scaled * scaled
    return 1.0 + squared * squared * (-35.0 + scaled * (84.0 + scaled * (-70.0 + scaled * 20.0)))

def couplings(own_pos, own_shield, near_pos, near_shield, shifts, listed, itself):
    displace = near_pos[:, :, None, :] + shifts[:, :, None, None] - own_pos[:, None, :, None]
    dist_sq = lax.optimization_barrier(jnp.sum(displace * displace, axis=0))
    distance = jnp.sqrt(dist_sq)
    screen = own_shield[None, :, None] * near_shield[:, None, :]
    kernel = COULOMB * taper_value(distance) / jnp.cbrt(dist_sq * distance + screen)
    diagonal_mask = jnp.eye(own_pos.shape[1], dtype=bool)
    retained = listed[:, None, None] & (distance < CUTOFF) & jnp.logical_not(itself[:, None, None] & diagonal_mask[None])
    return jnp.where(retained, kernel, jnp.zeros_like(kernel))

def table_lookup(type_ids, table):
    result = jnp.zeros(type_ids.shape, table.dtype)
    for kind_index in range(table.shape[0]):
        result = jnp.where(type_ids == kind_index, table[kind_index], result)
    return result

def decode_cells(entries, local_one, local_two, local_three, width_two, width_three):
    plane_cells = (width_two + 2) * (width_three + 2)
    step_one = entries // plane_cells - 1 - local_one[..., None]
    step_two = entries // (width_three + 2) % (width_two + 2) - 1 - local_two[..., None]
    step_three = entries % (width_three + 2) - 1 - local_three[..., None]
    return (step_one, step_two, step_three)

def reference(offsets, type_ids, neighbours, type_chi, type_eta, type_gamma):
    tiles = NCX * NCY * NCZ
    sentinel = (CX + 2) * (CY + 2) * (CZ + 2)
    shape_grid = (NCX, NCY, NCZ)
    grid_one = jnp.broadcast_to(jnp.arange(NCX, dtype=jnp.int32)[:, None, None], shape_grid)
    grid_two = jnp.broadcast_to(jnp.arange(NCY, dtype=jnp.int32)[None, :, None], shape_grid)
    grid_three = jnp.broadcast_to(jnp.arange(NCZ, dtype=jnp.int32)[None, None, :], shape_grid)
    step_one, step_two, step_three = decode_cells(neighbours, grid_one % CX, grid_two % CY, grid_three % CZ, CY, CZ)
    listed = neighbours != sentinel
    itself = (step_one == 0) & (step_two == 0) & (step_three == 0)
    target = ((grid_one[..., None] + step_one) % NCX * NCY + (grid_two[..., None] + step_two) % NCY) * NCZ + (grid_three[..., None] + step_three) % NCZ
    target = jnp.where(listed, target, tiles).astype(jnp.int32).reshape(tiles, NB)
    shifts = jnp.stack([step_one, step_two, step_three], axis=-2).reshape(tiles, 3, NB).astype(jnp.float32) * CELL_EDGE
    listed = listed.reshape(tiles, NB)
    itself = itself.reshape(tiles, NB)
    chi_atom = table_lookup(type_ids, type_chi).reshape(tiles, ATOMS)
    eta_atom = table_lookup(type_ids, type_eta).reshape(tiles, ATOMS)
    shield = table_lookup(type_ids, type_gamma ** (-1.5)).reshape(tiles, ATOMS)
    positions = offsets.reshape(3, tiles, ATOMS)
    pos_all = jnp.concatenate([positions, jnp.zeros((3, 1, ATOMS), positions.dtype)], 1)
    shield_all = jnp.concatenate([shield, jnp.zeros((1, ATOMS), shield.dtype)], 0)
    own_pos = jnp.moveaxis(positions, 1, 0)
    batch_size = 16
    rounds = tiles // batch_size

    def grouped(stacked):
        return stacked.reshape((rounds, batch_size) + stacked.shape[1:])
    inputs = (grouped(own_pos), grouped(shield), grouped(target), grouped(shifts), grouped(listed), grouped(itself))
    build_batch = jax.vmap(couplings)

    def tile_pass(vectors):
        padded = jnp.concatenate([vectors, jnp.zeros((2, 1, ATOMS), vectors.dtype)], 1)

        def one_round(tile_item):
            own_block, own_screen, row_index, shifted, valid_slot, selfish = tile_item
            near_block = jnp.moveaxis(pos_all[:, row_index], 0, 1)
            near_screen = shield_all[row_index]
            blocks = build_batch(own_block, own_screen, near_block, near_screen, shifted, valid_slot, selfish)
            values = padded[:, row_index]
            return jnp.einsum('bsij,cbsj->cbi', blocks, values, precision=lax.Precision.HIGHEST)
        products = lax.map(one_round, inputs)
        return jnp.moveaxis(products, 1, 0).reshape(2, tiles, ATOMS)
    source = jnp.stack([-chi_atom, -jnp.ones_like(chi_atom)])
    diagonal = eta_atom
    solution = jnp.zeros_like(source)
    residual = source
    direction = source
    norm_now = lax.optimization_barrier(jnp.sum(residual * residual, axis=(1, 2)))
    for iteration in range(ITERS):
        coupled = tile_pass(direction)
        image_now = diagonal[None] * direction + coupled
        step_size = norm_now / lax.optimization_barrier(jnp.sum(direction * image_now, axis=(1, 2)))
        solution = solution + step_size[:, None, None] * direction
        residual = residual - step_size[:, None, None] * image_now
        norm_next = lax.optimization_barrier(jnp.sum(residual * residual, axis=(1, 2)))
        direction = residual + (norm_next / norm_now)[:, None, None] * direction
        norm_now = norm_next
    level_ratio = jnp.sum(solution[0]) / jnp.sum(solution[1])
    charges = (1000.0 * (solution[0] - level_ratio * solution[1])).reshape(NCX, NCY, NCZ, ATOMS)
    return (charges, residual.reshape(2, NCX, NCY, NCZ, ATOMS))
```

```python
import functools

import jax
import jax.numpy as jnp
from jax import lax
from jax.experimental import pallas as pl
from jax.experimental.pallas import tpu as pltpu
from jax.sharding import Mesh
from jax.sharding import PartitionSpec as P

GX = ("gx_0", "gx_1")
GZ = ("gz_0", "gz_1")
PLANE = ("gx_0", "gx_1", "gy")
GROUP_ONE = ("gx_0", "gx_1", "gz_1")
GROUP_TWO = ("gy", "gz_0")

CELL_EDGE = 11.0
CUTOFF = 10.0
COULOMB = 14.4
FAR = 1.0e4
ATOMS = 128
SLOTS = 27
FIELDS = 4
SHIFTS = (200.0, 100.0, 20.0)
DISPLACED = tuple((a, b, c) for a in (-1, 0, 1) for b in (-1, 0, 1) for c in (-1, 0, 1))
VMEM = pltpu.VMEM
F32 = jnp.float32


def call(body, outs, scratch=()):
    return pl.pallas_call(
        body,
        out_shape=tuple(jax.ShapeDtypeStruct(s, F32) for s in outs),
        out_specs=tuple(pl.BlockSpec(memory_space=VMEM) for _ in outs),
        scratch_shapes=list(scratch),
        compiler_params=pltpu.CompilerParams(vmem_limit_bytes=48 * 2**20),
    )


def vmem():
    return pl.BlockSpec(memory_space=VMEM)


def run(body, outs, args, specs=None, scratch=()):
    specs = specs or [vmem() for _ in args]
    return pl.pallas_call(
        body,
        out_shape=tuple(jax.ShapeDtypeStruct(s, F32) for s in outs),
        in_specs=specs,
        out_specs=tuple(vmem() for _ in outs),
        scratch_shapes=list(scratch),
        compiler_params=pltpu.CompilerParams(vmem_limit_bytes=48 * 2**20),
    )(*args)


def pack_body(offsets, type_ids, own, head, tail):
    for c in range(2):
        for b in range(2):
            row = (c * 2 + b) * FIELDS
            for axis in range(3):
                local = 0.0 if axis == 0 else CELL_EDGE * (b if axis == 1 else c)
                own[row + axis : row + axis + 1, :] = offsets[axis, 0, b, c : c + 1, :] + local
            own[row + 3 : row + 4, :] = type_ids[0, b, c : c + 1, :].astype(F32)
    head[...] = own[0:8, :]
    tail[...] = own[8:16, :]


def lookup(kinds, table):
    return jnp.where(kinds == 0.0, table[0], table[1])


def shield_of(kinds, gamma):
    value = lookup(kinds, gamma)
    return 1.0 / (value * jnp.sqrt(value))


def own_body(own, neighbours, gamma, columns, penalty):
    for b in range(2):
        for c in range(2):
            tile = b * 2 + c
            for field in range(FIELDS):
                row = (c * 2 + b) * FIELDS + field
                values = own[row : row + 1, :]
                if field == 3:
                    values = shield_of(values, gamma)
                columns[tile, field] = jnp.broadcast_to(values, (ATOMS, ATOMS)).T
            listed = neighbours[0, b, c : c + 1, :]
            slot = lax.broadcasted_iota(jnp.int32, (SLOTS, SLOTS), 0)
            one = jnp.where(slot >= 9, 1, 0) + jnp.where(slot >= 18, 1, 0)
            rest = slot - 9 * one
            two = jnp.where(rest >= 3, 1, 0) + jnp.where(rest >= 6, 1, 0)
            three = rest - 3 * two
            index = one * 16 + (two + b) * 4 + three + c
            found = jnp.max(jnp.where(listed == index, 1.0, 0.0), axis=1, keepdims=True)
            penalty[tile] = jnp.broadcast_to(jnp.where(found > 0.0, 0.0, FAR), (SLOTS, ATOMS))


def plane_position():
    first = lax.axis_index("gx_0") * 2 + lax.axis_index("gx_1")
    return first, lax.axis_index("gy")


def columns_of_plane():
    first, second = plane_position()
    for ix in range(3):
        for iy in range(4):
            step = -1 if iy == 0 else (1 if iy == 3 else 0)
            peer = ((first + ix + 3) % 4) * 4 + (second + step + 4) % 4
            yield ix, iy, peer, (iy + 1) % 2, step


def row_sums(acc):
    return jnp.sum(acc.T, axis=0, keepdims=True)


def build_body(
    received, columns, penalty, chi, eta, gamma, blocks, out, head, tail, near, acc
):
    for ix, iy, peer, b, step in columns_of_plane():
        for iz in range(4):
            p = (ix * 4 + iy) * 4 + iz
            row = (iz * 2 + b) * FIELDS
            cell = (received[peer, row + k : row + k + 1, :] for k in range(FIELDS))
            x, y, z, kinds = (jnp.broadcast_to(v, (8, ATOMS)) for v in cell)
            near[0, p] = x + CELL_EDGE * (ix - 1)
            near[1, p] = y + CELL_EDGE * 2 * step
            near[2, p] = z + (-2 * CELL_EDGE if iz == 0 else (2 * CELL_EDGE if iz == 3 else 0.0))
            near[3, p] = shield_of(kinds, gamma)
            near[4, p] = lookup(kinds, chi)

    half_rows = ATOMS // 2
    groups = half_rows // 8
    lane = lax.broadcasted_iota(jnp.int32, (8, ATOMS), 1)
    sub = lax.broadcasted_iota(jnp.int32, (8, ATOMS), 0)
    ratio = COULOMB / CUTOFF**7

    def half_tile(step, carry):
        tile = step // 2
        start = (step % 2) * half_rows
        base = 16 + (tile // 2 + 1) * 4 + tile % 2 + 1
        sums_s = [jnp.zeros((8, ATOMS), F32) for _ in range(groups)]
        sums_t = [jnp.zeros((8, ATOMS), F32) for _ in range(groups)]
        for d, (da, db, dc) in enumerate(DISPLACED):
            p = base + da * 16 + db * 4 + dc
            away = penalty[tile, d : d + 1, :]
            xj = near[0, p] + away
            yj, zj, sj, cj = near[1, p], near[2, p], near[3, p], near[4, p]
            for g in range(groups):
                rows = pl.ds(pl.multiple_of(start + g * 8, 8), 8)
                dx = xj - columns[tile, 0, rows, :]
                dy = yj - columns[tile, 1, rows, :]
                dz = zj - columns[tile, 2, rows, :]
                r2 = dx * dx + dy * dy + dz * dz
                r = r2 * lax.rsqrt(r2)
                x = r2 * r + columns[tile, 3, rows, :] * sj
                inverse = jnp.exp2(jnp.log(x) * (-1.0 / (3.0 * 0.6931471805599453)))
                w = jnp.maximum(CUTOFF - r, 0.0)
                w2 = w * w
                taper = (w2 * w2) * (
                    35.0e3 * ratio + w * (-84.0e2 * ratio + w * (70.0e1 * ratio + w * (-20.0 * ratio)))
                )
                value = taper * inverse
                if d == 13:
                    value = jnp.where(lane == sub + (start + g * 8), 0.0, value)
                blocks[tile, d, rows, :] = value
                sums_t[g] = sums_t[g] + value
                sums_s[g] = sums_s[g] + value * cj
        for g in range(groups):
            rows = pl.ds(pl.multiple_of(start + g * 8, 8), 8)
            acc[tile, 0, rows, :] = sums_s[g]
            acc[tile, 1, rows, :] = sums_t[g]
        return carry

    lax.fori_loop(0, 8, half_tile, 0)
    first, second = plane_position()
    me = first * 4 + second
    for c in range(2):
        for b in range(2):
            tile = b * 2 + c
            kinds = received[me, (((c + 1) * 2 + b) * FIELDS + 3) : (((c + 1) * 2 + b) * FIELDS + 4), :]
            shifted = lookup(kinds, eta) - SHIFTS[0]
            row = (c * 2 + b) * 2
            out[row : row + 1, :] = -(shifted * lookup(kinds, chi) + row_sums(acc[tile, 0]))
            out[row + 1 : row + 2, :] = -(shifted + row_sums(acc[tile, 1]))
    head[...] = out[0:4, :]
    tail[...] = out[4:8, :]


def image_rows(received, blocks, near, acc):
    for ix, iy, peer, b, step in columns_of_plane():
        for iz in range(4):
            p = (ix * 4 + iy) * 4 + iz
            for system in range(2):
                row = (iz * 2 + b) * 2 + system
                near[system, p] = jnp.broadcast_to(received[peer, row : row + 1, :], (8, ATOMS))
    half_rows = ATOMS // 2
    groups = half_rows // 8

    def half_tile(step, carry):
        tile = step // 2
        start = (step % 2) * half_rows
        base = 16 + (tile // 2 + 1) * 4 + tile % 2 + 1
        sums_s = [jnp.zeros((8, ATOMS), F32) for _ in range(groups)]
        sums_t = [jnp.zeros((8, ATOMS), F32) for _ in range(groups)]
        for d, (da, db, dc) in enumerate(DISPLACED):
            p = base + da * 16 + db * 4 + dc
            vs, vt = near[0, p], near[1, p]
            for g in range(groups):
                rows = pl.ds(pl.multiple_of(start + g * 8, 8), 8)
                value = blocks[tile, d, rows, :]
                sums_s[g] = sums_s[g] + value * vs
                sums_t[g] = sums_t[g] + value * vt
        for g in range(groups):
            rows = pl.ds(pl.multiple_of(start + g * 8, 8), 8)
            acc[tile, 0, rows, :] = sums_s[g]
            acc[tile, 1, rows, :] = sums_t[g]
        return carry

    lax.fori_loop(0, 8, half_tile, 0)


def next_vector(fields, eta, vector, acc, out, shift):
    for c in range(2):
        for b in range(2):
            tile = b * 2 + c
            row = (c * 2 + b) * FIELDS + 3
            shifted = lookup(fields[row : row + 1, :], eta) - shift
            for system in range(2):
                line = (c * 2 + b) * 2 + system
                out[line : line + 1, :] = shifted * vector[line : line + 1, :] + row_sums(
                    acc[tile, system]
                )


def second_body(received, blocks, fields, vector, eta, out, head, tail, near, acc):
    image_rows(received, blocks, near, acc)
    next_vector(fields, eta, vector, acc, out, SHIFTS[1])
    head[...] = out[0:4, :]
    tail[...] = out[4:8, :]


def source_rows(fields, chi):
    rows = []
    for cell in range(4):
        kinds = fields[cell * FIELDS + 3 : cell * FIELDS + 4, :]
        rows.append(-lookup(kinds, chi))
        rows.append(jnp.full((1, ATOMS), -1.0, F32))
    return jnp.concatenate(rows, axis=0)


def third_body(received, blocks, fields, w1, w2, chi, eta, out, sums, near, acc, moments):
    image_rows(received, blocks, near, acc)
    next_vector(fields, eta, w2, acc, out, SHIFTS[2])
    v0, v1, v2, v3 = source_rows(fields, chi), w1[...], w2[...], out[...]
    moments[...] = jnp.zeros((ATOMS, ATOMS), F32)
    pairs = (v0 * v0, v0 * v1, v0 * v2, v1 * v1, v1 * v2, v2 * v2, v2 * v3, v0, v1, v2)
    for k, item in enumerate(pairs):
        moments[2 * k : 2 * k + 2, :] = (item[0:2] + item[2:4]) + (item[4:6] + item[6:8])
    sums[...] = row_sums(moments[...])


def last_body(received, fields, w1, w2, w3, chi, charges, residuals):
    total = jnp.sum(received[...], axis=0)
    spread = jnp.broadcast_to(total, (ATOMS, ATOMS)).T
    g00, g01, g02, g11, g12, g22, g23, s0, s1, s2 = (spread[2 * k : 2 * k + 2, :] for k in range(10))
    shift0, shift1, shift2 = SHIFTS
    a00 = g01 + shift0 * g00
    a01 = g11 + shift0 * g01
    a02 = g12 + shift0 * g02
    a11 = g12 + shift1 * g11
    a12 = g22 + shift1 * g12
    a22 = g23 + shift2 * g22
    l10 = a01 / a00
    l20 = a02 / a00
    b11 = a11 - l10 * a01
    b12 = a12 - l10 * a02
    b22 = a22 - l20 * a02
    l21 = b12 / b11
    pivot = b22 - l21 * b12
    y1 = g01 - l10 * g00
    y2 = g02 - l20 * g00 - l21 * y1
    c2 = y2 / pivot
    c1 = (y1 - b12 * c2) / b11
    c0 = (g00 - a01 * c1 - a02 * c2) / a00
    level = c0 * s0 + c1 * s1 + c2 * s2
    level = level[0:1] / level[1:2]

    def every(value):
        return jnp.concatenate([value] * 4, axis=0)

    v0, v1, v2, v3 = source_rows(fields, chi), w1[...], w2[...], w3[...]
    solution_rows = every(c0) * v0 + every(c1) * v1 + every(c2) * v2
    residual_rows = (
        every(1.0 - shift0 * c0) * v0
        - every(c0 + shift1 * c1) * v1
        - every(c1 + shift2 * c2) * v2
        - every(c2) * v3
    )
    for c in range(2):
        for b in range(2):
            row = (c * 2 + b) * 2
            charges[0, b, c : c + 1, :] = 1000.0 * (
                solution_rows[row : row + 1] - level * solution_rows[row + 1 : row + 2]
            )
            for system in range(2):
                residuals[system, 0, b, c : c + 1, :] = residual_rows[row + system : row + system + 1]


def surrounded(own, head, tail):
    count = lax.axis_size(GZ)
    below = lax.ppermute(tail, GZ, [(i, (i + 1) % count) for i in range(count)])
    above = lax.ppermute(head, GZ, [((i + 1) % count, i) for i in range(count)])
    block = jnp.concatenate([below, own, above], axis=0)
    return lax.all_to_all(
        jnp.broadcast_to(block[None], (16,) + block.shape), PLANE, 0, 0, tiled=True
    )


def shared(row, axes):
    return lax.all_to_all(
        jnp.broadcast_to(row[None], (lax.axis_size(axes),) + row.shape), axes, 0, 0, tiled=True
    )


def per_device(offsets, type_ids, neighbours, type_chi, type_eta, type_gamma):
    smem = pl.BlockSpec(memory_space=pltpu.SMEM)
    fields, head, tail = run(pack_body, [(16, ATOMS), (8, ATOMS), (8, ATOMS)], (offsets, type_ids))
    columns, penalty = run(
        own_body,
        [(4, FIELDS, ATOMS, ATOMS), (4, SLOTS, ATOMS)],
        (fields, neighbours, type_gamma),
        [vmem(), vmem(), smem],
    )
    received = surrounded(fields, head, tail)
    matrix = (4, SLOTS, ATOMS, ATOMS)
    accumulate = VMEM((4, 2, ATOMS, ATOMS), F32)
    vectors = [(8, ATOMS), (4, ATOMS), (4, ATOMS)]
    blocks, w1, head, tail = run(
        build_body,
        [matrix] + vectors,
        (received, columns, penalty, type_chi, type_eta, type_gamma),
        [vmem(), vmem(), vmem(), smem, smem, smem],
        [VMEM((5, 48, 8, ATOMS), F32), accumulate],
    )
    near = VMEM((2, 48, 8, ATOMS), F32)
    received = surrounded(w1, head, tail)
    w2, head, tail = run(
        second_body,
        vectors,
        (received, blocks, fields, w1, type_eta),
        [vmem(), vmem(), vmem(), vmem(), smem],
        [near, accumulate],
    )
    received = surrounded(w2, head, tail)
    w3, sums = run(
        third_body,
        [(8, ATOMS), (1, ATOMS)],
        (received, blocks, fields, w1, w2, type_chi, type_eta),
        [vmem(), vmem(), vmem(), vmem(), vmem(), smem, smem],
        [near, accumulate, VMEM((ATOMS, ATOMS), F32)],
    )
    partial = jnp.sum(shared(sums, GROUP_ONE), axis=0)
    received = shared(partial, GROUP_TWO)
    return run(
        last_body,
        [(1, 2, 2, ATOMS), (2, 1, 2, 2, ATOMS)],
        (received, fields, w1, w2, w3, type_chi),
        [vmem(), vmem(), vmem(), vmem(), vmem(), smem],
    )


def solution(mesh):
    torus = Mesh(
        mesh.devices.reshape(2, 2, mesh.shape["gy"], 8, 8), ("gx_0", "gx_1", "gy", "gz_0", "gz_1")
    )
    in_specs = (
        P(None, GX, "gy", GZ, None),
        P(GX, "gy", GZ, None),
        P(GX, "gy", GZ, None),
        P(),
        P(),
        P(),
    )
    out_specs = (P(GX, "gy", GZ, None), P(None, GX, "gy", GZ, None))
    return jax.shard_map(
        per_device, mesh=torus, in_specs=in_specs, out_specs=out_specs, check_vma=False
    )
```

```python
import functools

import jax
import jax.numpy as jnp
from jax import lax
from jax.experimental import pallas as pl
from jax.experimental.pallas import tpu as pltpu
from jax.sharding import Mesh
from jax.sharding import PartitionSpec as P

GX = ("gx_0", "gx_1")
GZ = ("gz_0", "gz_1")
PLANE = ("gx_0", "gx_1", "gy")
GROUP_ONE = ("gx_0", "gx_1", "gz_1")
GROUP_TWO = ("gy", "gz_0")

CELL_EDGE = 11.0
CUTOFF = 10.0
SCALE = 14.4 * 0.02 / CUTOFF**4
FAR = 1.0e4
ATOMS = 128
GROUPS = 8
FIELDS = 4
SHIFTS = (200.0, 100.0, 20.0)
INNER = tuple((ix, jy, k) for ix in range(3) for jy in range(3) for k in range(2))
OUTER = tuple((ix, jy) for ix in range(3) for jy in range(3))
VMEM = pltpu.VMEM
HBM = pltpu.HBM
F32 = jnp.float32


def run(body, outs, args, spaces=None, scratch=()):
    spaces = spaces or [VMEM] * len(args)
    held = [
        pltpu.with_memory_space_constraint(x, VMEM if space == VMEM else HBM)
        for x, space in zip(args, spaces)
    ]
    return pl.pallas_call(
        body,
        out_shape=tuple(VMEM(shape, F32) for shape in outs),
        in_specs=[pl.BlockSpec(memory_space=space) for space in spaces],
        out_specs=tuple(pl.BlockSpec(memory_space=VMEM) for _ in outs),
        scratch_shapes=list(scratch),
        compiler_params=pltpu.CompilerParams(vmem_limit_bytes=12 * 2**20),
    )(*held)


def pack_body(offsets_far, types_far, own, offsets, type_ids, one, two):
    first = pltpu.make_async_copy(offsets_far, offsets, one)
    second = pltpu.make_async_copy(types_far, type_ids, two)
    first.start()
    second.start()
    first.wait()
    second.wait()
    for c in range(2):
        for b in range(2):
            row = (c * 2 + b) * FIELDS
            for axis in range(3):
                local = 0.0 if axis == 0 else CELL_EDGE * (b if axis == 1 else c)
                own[row + axis : row + axis + 1, :] = offsets[axis, 0, b, c : c + 1, :] + local
            own[row + 3 : row + 4, :] = type_ids[0, b, c : c + 1, :].astype(F32)


def plane_columns():
    first = lax.axis_index("gx_0") * 2 + lax.axis_index("gx_1")
    second = lax.axis_index("gy")
    for ix in range(3):
        for iy in range(4):
            step = -1 if iy == 0 else (1 if iy == 3 else 0)
            peer = ((first + ix + 3) % 4) * 4 + (second + step + 4) % 4
            yield ix, iy, peer, (iy + 1) % 2, step


def faces_body(received, head, tail):
    for ix, iy, peer, b, step in plane_columns():
        for face, c in ((head, 0), (tail, 1)):
            row = (c * 2 + b) * FIELDS
            line = (ix * 4 + iy) * FIELDS
            face[line : line + 1, :] = received[peer, row : row + 1, :] + CELL_EDGE * (ix - 1)
            face[line + 1 : line + 2, :] = received[peer, row + 1 : row + 2, :] + CELL_EDGE * 2 * step
            face[line + 2 : line + 4, :] = received[peer, row + 2 : row + 4, :]


def choose(kinds, table, first):
    return jnp.where(kinds == 0.0, table[first : first + 1, :], table[first + 1 : first + 2, :])


def place(near, index, lines, table, lift):
    x, y, z, kinds = (jnp.broadcast_to(v, (8, ATOMS)) for v in lines)
    near[0, index] = x
    near[1, index] = y
    near[2, index] = z + lift
    near[3, index] = choose(kinds, table, 0)
    near[4, index] = choose(kinds, table, 2)


def row_sums(acc):
    return jnp.sum(acc.T, axis=0, keepdims=True)


def couple(near, columns, away, tile, start, p, line, blocks, slot, sums_s, sums_t, mask):
    xj = near[0, p] + away[tile, line : line + 1, :]
    yj, zj, sj, cj = near[1, p], near[2, p], near[3, p], near[4, p]
    for g in range(GROUPS):
        rows = pl.ds(pl.multiple_of(start + g * 8, 8), 8)
        dx = xj - columns[tile, 0, rows, :]
        dy = yj - columns[tile, 1, rows, :]
        dz = zj - columns[tile, 2, rows, :]
        r2 = dx * dx + dy * dy + dz * dz
        r = r2 * lax.rsqrt(r2)
        x = r2 * r + columns[tile, 3, rows, :] * sj
        inverse = jnp.exp2(lax.log2(x) * (-1.0 / 3.0))
        w = jnp.maximum(CUTOFF - r, 0.0)
        w2 = w * w
        value = (w2 * w2) * (((r + 5.0) * r + 20.0) * r + 50.0) * inverse
        if mask is not None:
            value = jnp.where(mask(g), 0.0, value)
        blocks[tile, slot, rows, :] = value
        sums_t[g] = sums_t[g] + value
        sums_s[g] = sums_s[g] + value * cj


def store(acc, tile, start, sums_s, sums_t):
    for g in range(GROUPS):
        rows = pl.ds(pl.multiple_of(start + g * 8, 8), 8)
        acc[tile, 0, rows, :] = sums_s[g]
        acc[tile, 1, rows, :] = sums_t[g]


def listed(entries, index):
    found = jnp.max(jnp.where(entries == index, 1.0, 0.0), axis=1, keepdims=True)
    return jnp.broadcast_to(jnp.where(found > 0.0, 0.0, FAR), (index.shape[0], ATOMS))


def split(number, by, parts):
    high = sum(jnp.where(number >= by * k, 1, 0) for k in range(1, parts))
    return high, number - by * high


def inner_body(
    received, own, neighbours, chi, eta, gamma, face,
    blocks, acc, columns, away_outer, table, face_out, near, away,
):
    for kind in range(2):
        value = jnp.full((1, ATOMS), gamma[kind], F32)
        table[kind : kind + 1, :] = 1.0 / (value * jnp.sqrt(value))
        table[2 + kind : 3 + kind, :] = jnp.full((1, ATOMS), chi[kind], F32)
        table[4 + kind : 5 + kind, :] = jnp.full((1, ATOMS), eta[kind], F32)
    face_out[...] = face[...]
    for b in range(2):
        for c in range(2):
            tile = b * 2 + c
            for field in range(FIELDS):
                row = (c * 2 + b) * FIELDS + field
                values = own[row : row + 1, :]
                if field == 3:
                    values = choose(values, table, 0)
                columns[tile, field] = jnp.broadcast_to(values, (ATOMS, ATOMS)).T
            entries = neighbours[0, b, c : c + 1, :]
            slot = lax.broadcasted_iota(jnp.int32, (18, 27), 0)
            ix, rest = split(slot, 6, 3)
            jy, k = split(rest, 2, 3)
            away[tile] = listed(entries, ix * 16 + (jy + b) * 4 + k + 1)
            slot = lax.broadcasted_iota(jnp.int32, (9, 27), 0)
            ix, jy = split(slot, 3, 3)
            away_outer[tile] = listed(entries, ix * 16 + (jy + b) * 4 + 3 * c)
    for ix, iy, peer, b, step in plane_columns():
        for k in range(2):
            row = (k * 2 + b) * FIELDS
            lines = [received[peer, row + f : row + f + 1, :] for f in range(FIELDS)]
            lines[0] = lines[0] + CELL_EDGE * (ix - 1)
            lines[1] = lines[1] + CELL_EDGE * 2 * step
            place(near, (ix * 4 + iy) * 2 + k, lines, table, 0.0)

    lane = lax.broadcasted_iota(jnp.int32, (8, ATOMS), 1)
    sub = lax.broadcasted_iota(jnp.int32, (8, ATOMS), 0)

    def half_tile(step, carry):
        tile = step // 2
        b, c = tile // 2, tile % 2
        start = (step % 2) * (GROUPS * 8)
        sums_s = [jnp.zeros((8, ATOMS), F32) for _ in range(GROUPS)]
        sums_t = [jnp.zeros((8, ATOMS), F32) for _ in range(GROUPS)]
        for slot, (ix, jy, k) in enumerate(INNER):
            mask = None
            if (ix, jy) == (1, 1):
                first = start + jnp.where(c == k, 0, 2 * ATOMS)
                mask = functools.partial(lambda at, g: lane == sub + (at + g * 8), first)
            p = (ix * 4 + jy + b) * 2 + k
            couple(near, columns, away, tile, start, p, slot, blocks, slot, sums_s, sums_t, mask)
        store(acc, tile, start, sums_s, sums_t)
        return carry

    lax.fori_loop(0, 8, half_tile, 0)


def outer_body(
    below, above, own, columns, away, table, partial,
    blocks, out, head, tail, near, acc,
):
    for ix in range(3):
        for iy in range(4):
            line = (ix * 4 + iy) * FIELDS
            for side, (ghost, lift) in enumerate(((below, -2 * CELL_EDGE), (above, 2 * CELL_EDGE))):
                lines = [ghost[line + f : line + f + 1, :] for f in range(FIELDS)]
                place(near, (ix * 4 + iy) * 2 + side, lines, table, lift)

    def half_tile(step, carry):
        tile = step // 2
        b, c = tile // 2, tile % 2
        start = (step % 2) * (GROUPS * 8)
        rows = [pl.ds(pl.multiple_of(start + g * 8, 8), 8) for g in range(GROUPS)]
        sums_s = [partial[tile, 0, r, :] for r in rows]
        sums_t = [partial[tile, 1, r, :] for r in rows]
        for slot, (ix, jy) in enumerate(OUTER):
            p = (ix * 4 + jy + b) * 2 + c
            couple(near, columns, away, tile, start, p, slot, blocks, slot, sums_s, sums_t, None)
        store(acc, tile, start, sums_s, sums_t)
        return carry

    lax.fori_loop(0, 8, half_tile, 0)
    source = source_rows(own, table)
    next_vector(own, table, source, acc, out, SHIFTS[0], (-SCALE, -SCALE))
    head[...] = out[0:4, :]
    tail[...] = out[4:8, :]


def image_rows(received, inner, outer, near, acc):
    for ix, iy, peer, b, step in plane_columns():
        for iz in range(4):
            for system in range(2):
                row = (iz * 2 + b) * 2 + system
                near[system, (ix * 4 + iy) * 4 + iz] = jnp.broadcast_to(
                    received[peer, row : row + 1, :], (8, ATOMS)
                )
    groups = ATOMS // 8

    def one_tile(tile, carry):
        b, c = tile // 2, tile % 2
        sums_s = [jnp.zeros((8, ATOMS), F32) for _ in range(groups)]
        sums_t = [jnp.zeros((8, ATOMS), F32) for _ in range(groups)]
        places = [((ix * 4 + jy + b) * 4 + k + 1, inner, n) for n, (ix, jy, k) in enumerate(INNER)]
        places += [((ix * 4 + jy + b) * 4 + 3 * c, outer, n) for n, (ix, jy) in enumerate(OUTER)]
        for p, blocks, slot in places:
            vs, vt = near[0, p], near[1, p]
            for g in range(groups):
                value = blocks[tile, slot, g * 8 : g * 8 + 8, :]
                sums_s[g] = sums_s[g] + value * vs
                sums_t[g] = sums_t[g] + value * vt
        for g in range(groups):
            acc[tile, 0, g * 8 : g * 8 + 8, :] = sums_s[g]
            acc[tile, 1, g * 8 : g * 8 + 8, :] = sums_t[g]
        return carry

    lax.fori_loop(0, 4, one_tile, 0)


def next_vector(own, table, vector, acc, out, shift, scales=(SCALE, SCALE)):
    for c in range(2):
        for b in range(2):
            tile = b * 2 + c
            kind = (c * 2 + b) * FIELDS + 3
            shifted = choose(own[kind : kind + 1, :], table, 4) - shift
            for system in range(2):
                line = (c * 2 + b) * 2 + system
                out[line : line + 1, :] = shifted * vector[line : line + 1, :] + scales[
                    system
                ] * row_sums(acc[tile, system])


def second_body(received, inner, outer, own, table, vector, out, head, tail, near, acc):
    image_rows(received, inner, outer, near, acc)
    next_vector(own, table, vector, acc, out, SHIFTS[1])
    head[...] = out[0:4, :]
    tail[...] = out[4:8, :]


def source_rows(own, table):
    rows = []
    for cell in range(4):
        kind = cell * FIELDS + 3
        rows.append(-choose(own[kind : kind + 1, :], table, 2))
        rows.append(jnp.full((1, ATOMS), -1.0, F32))
    return jnp.concatenate(rows, axis=0)


def third_body(received, inner, outer, own, table, w1, w2, out, sums, near, acc, moments):
    image_rows(received, inner, outer, near, acc)
    next_vector(own, table, w2, acc, out, SHIFTS[2])
    v0, v1, v2, v3 = source_rows(own, table), w1[...], w2[...], out[...]
    moments[...] = jnp.zeros((ATOMS, ATOMS), F32)
    pairs = (v0 * v0, v0 * v1, v0 * v2, v1 * v1, v1 * v2, v2 * v2, v2 * v3, v0, v1, v2)
    for k, item in enumerate(pairs):
        moments[2 * k : 2 * k + 2, :] = (item[0:2] + item[2:4]) + (item[4:6] + item[6:8])
    sums[...] = row_sums(moments[...])


def last_body(received, own, table, w1, w2, w3, charges, residuals):
    total = jnp.sum(received[...], axis=0)
    spread = jnp.broadcast_to(total, (ATOMS, ATOMS)).T
    g00, g01, g02, g11, g12, g22, g23, s0, s1, s2 = (spread[2 * k : 2 * k + 2, :] for k in range(10))
    shift0, shift1, shift2 = SHIFTS
    a00 = g01 + shift0 * g00
    a01 = g11 + shift0 * g01
    a02 = g12 + shift0 * g02
    a11 = g12 + shift1 * g11
    a12 = g22 + shift1 * g12
    a22 = g23 + shift2 * g22
    l10 = a01 / a00
    l20 = a02 / a00
    b11 = a11 - l10 * a01
    b12 = a12 - l10 * a02
    b22 = a22 - l20 * a02
    l21 = b12 / b11
    pivot = b22 - l21 * b12
    y1 = g01 - l10 * g00
    y2 = g02 - l20 * g00 - l21 * y1
    c2 = y2 / pivot
    c1 = (y1 - b12 * c2) / b11
    c0 = (g00 - a01 * c1 - a02 * c2) / a00
    level = c0 * s0 + c1 * s1 + c2 * s2
    level = level[0:1] / level[1:2]

    def every(value):
        return jnp.concatenate([value] * 4, axis=0)

    v0, v1, v2, v3 = source_rows(own, table), w1[...], w2[...], w3[...]
    solution_rows = every(c0) * v0 + every(c1) * v1 + every(c2) * v2
    residual_rows = (
        every(1.0 - shift0 * c0) * v0
        - every(c0 + shift1 * c1) * v1
        - every(c1 + shift2 * c2) * v2
        - every(c2) * v3
    )
    for c in range(2):
        for b in range(2):
            row = (c * 2 + b) * 2
            charges[0, b, c : c + 1, :] = 1000.0 * (
                solution_rows[row : row + 1] - level * solution_rows[row + 1 : row + 2]
            )
            for system in range(2):
                residuals[system, 0, b, c : c + 1, :] = residual_rows[row + system : row + system + 1]


def upward(tail):
    count = lax.axis_size(GZ)
    return lax.ppermute(tail, GZ, [(i, (i + 1) % count) for i in range(count)])


def downward(head):
    count = lax.axis_size(GZ)
    return lax.ppermute(head, GZ, [((i + 1) % count, i) for i in range(count)])


def shared(block, axes):
    count = lax.axis_size(axes)
    return lax.all_to_all(
        jnp.broadcast_to(block[None], (count,) + block.shape), axes, 0, 0, tiled=True
    )


def surrounded(own, head, tail):
    return shared(jnp.concatenate([upward(tail), own, downward(head)], axis=0), PLANE)


def per_device(offsets, type_ids, neighbours, type_chi, type_eta, type_gamma):
    smem = pltpu.SMEM
    (own,) = run(
        pack_body,
        [(16, ATOMS)],
        (offsets, type_ids),
        [HBM, HBM],
        [
            VMEM(offsets.shape, F32),
            VMEM(type_ids.shape, jnp.int32),
            pltpu.SemaphoreType.DMA,
            pltpu.SemaphoreType.DMA,
        ],
    )
    received = shared(own, PLANE)
    head, tail = run(faces_body, [(48, ATOMS), (48, ATOMS)], (received,))
    below = upward(tail)
    products = (4, 2, ATOMS, ATOMS)
    accumulate = VMEM(products, F32)
    inner, partial, columns, away, table, head = run(
        inner_body,
        [(4, 18, ATOMS, ATOMS), products, (4, FIELDS, ATOMS, ATOMS), (4, 9, ATOMS), (8, ATOMS), (48, ATOMS)],
        (received, own, neighbours, type_chi, type_eta, type_gamma, head),
        [VMEM, VMEM, VMEM, smem, smem, smem, VMEM],
        [VMEM((5, 24, 8, ATOMS), F32), VMEM((4, 18, ATOMS), F32)],
    )
    above = downward(head)
    vectors = [(8, ATOMS), (4, ATOMS), (4, ATOMS)]
    outer, w1, head, tail = run(
        outer_body,
        [(4, 9, ATOMS, ATOMS)] + vectors,
        (below, above, own, columns, away, table, partial),
        scratch=[VMEM((5, 24, 8, ATOMS), F32), accumulate],
    )
    near = VMEM((2, 48, 8, ATOMS), F32)
    received = surrounded(w1, head, tail)
    w2, head, tail = run(
        second_body, vectors, (received, inner, outer, own, table, w1), scratch=[near, accumulate]
    )
    received = surrounded(w2, head, tail)
    w3, sums = run(
        third_body,
        [(8, ATOMS), (1, ATOMS)],
        (received, inner, outer, own, table, w1, w2),
        scratch=[near, accumulate, VMEM((ATOMS, ATOMS), F32)],
    )
    half = jnp.sum(shared(sums, GROUP_ONE), axis=0)
    received = shared(half, GROUP_TWO)
    held = [pltpu.with_memory_space_constraint(x, VMEM) for x in (received, own, table, w1, w2, w3)]
    return pl.pallas_call(
        last_body,
        out_shape=(
            jax.ShapeDtypeStruct((1, 2, 2, ATOMS), F32),
            jax.ShapeDtypeStruct((2, 1, 2, 2, ATOMS), F32),
        ),
        in_specs=[pl.BlockSpec(memory_space=VMEM)] * 6,
        out_specs=(pl.BlockSpec(memory_space=VMEM),) * 2,
    )(*held)


def solution(mesh):
    torus = Mesh(
        mesh.devices.reshape(2, 2, mesh.shape["gy"], 8, 8), ("gx_0", "gx_1", "gy", "gz_0", "gz_1")
    )
    in_specs = (
        P(None, GX, "gy", GZ, None),
        P(GX, "gy", GZ, None),
        P(GX, "gy", GZ, None),
        P(),
        P(),
        P(),
    )
    out_specs = (P(GX, "gy", GZ, None), P(None, GX, "gy", GZ, None))
    return jax.shard_map(
        per_device, mesh=torus, in_specs=in_specs, out_specs=out_specs, check_vma=False
    )
```

```python
import functools

import jax
import jax.numpy as jnp
from jax import lax
from jax.experimental import pallas as pl
from jax.experimental.pallas import tpu as pltpu
from jax.sharding import Mesh
from jax.sharding import PartitionSpec as P

GX = ("gx_0", "gx_1")
GZ = ("gz_0", "gz_1")
PLANE = ("gx_0", "gx_1", "gy")
GROUP_ONE = ("gx_0", "gx_1", "gy", "gz_1")
GROUP_TWO = ("gz_0",)

CELL_EDGE = 11.0
CUTOFF = 10.0
SCALE = 14.4 * 0.02 / CUTOFF**4
FAR = 1.0e4
ATOMS = 128
GROUPS = 8
FIELDS = 4
SHIFTS = (200.0, 100.0, 20.0)
INNER = tuple((ix, jy, k) for ix in range(3) for jy in range(3) for k in range(2))
OUTER = tuple((ix, jy) for ix in range(3) for jy in range(3))
VMEM = pltpu.VMEM
HBM = pltpu.HBM
F32 = jnp.float32


def run(body, outs, args, spaces=None, scratch=()):
    spaces = spaces or [VMEM] * len(args)
    held = [
        pltpu.with_memory_space_constraint(x, VMEM if space == VMEM else HBM)
        for x, space in zip(args, spaces)
    ]
    return pl.pallas_call(
        body,
        out_shape=tuple(VMEM(shape, F32) for shape in outs),
        in_specs=[pl.BlockSpec(memory_space=space) for space in spaces],
        out_specs=tuple(pl.BlockSpec(memory_space=VMEM) for _ in outs),
        scratch_shapes=list(scratch),
        compiler_params=pltpu.CompilerParams(vmem_limit_bytes=12 * 2**20),
    )(*held)


def pack_body(offsets_far, types_far, own, offsets, type_ids, one, two):
    first = pltpu.make_async_copy(offsets_far, offsets, one)
    second = pltpu.make_async_copy(types_far, type_ids, two)
    first.start()
    second.start()
    first.wait()
    second.wait()
    for c in range(2):
        for b in range(2):
            row = (c * 2 + b) * FIELDS
            for axis in range(3):
                local = 0.0 if axis == 0 else CELL_EDGE * (b if axis == 1 else c)
                own[row + axis : row + axis + 1, :] = offsets[axis, 0, b, c : c + 1, :] + local
            own[row + 3 : row + 4, :] = type_ids[0, b, c : c + 1, :].astype(F32)


def plane_columns():
    first = lax.axis_index("gx_0") * 2 + lax.axis_index("gx_1")
    second = lax.axis_index("gy")
    for ix in range(3):
        for iy in range(4):
            step = -1 if iy == 0 else (1 if iy == 3 else 0)
            peer = ((first + ix + 3) % 4) * 4 + (second + step + 4) % 4
            yield ix, iy, peer, (iy + 1) % 2, step


def faces_body(received, head, tail):
    for ix, iy, peer, b, step in plane_columns():
        for face, c in ((head, 0), (tail, 1)):
            row = (c * 2 + b) * FIELDS
            line = (ix * 4 + iy) * FIELDS
            face[line : line + 1, :] = received[peer, row : row + 1, :] + CELL_EDGE * (ix - 1)
            face[line + 1 : line + 2, :] = received[peer, row + 1 : row + 2, :] + CELL_EDGE * 2 * step
            face[line + 2 : line + 4, :] = received[peer, row + 2 : row + 4, :]


def choose(kinds, table, first):
    return jnp.where(kinds == 0.0, table[first : first + 1, :], table[first + 1 : first + 2, :])


def place(near, index, lines, table, lift):
    x, y, z, kinds = (jnp.broadcast_to(v, (8, ATOMS)) for v in lines)
    near[0, index] = x
    near[1, index] = y
    near[2, index] = z + lift
    near[3, index] = choose(kinds, table, 0)
    near[4, index] = choose(kinds, table, 2)


def row_sums(acc):
    return jnp.sum(acc.T, axis=0, keepdims=True)


def couple(near, columns, away, tile, start, p, line, blocks, slot, sums_s, sums_t, mask):
    xj = near[0, p] + away[tile, line : line + 1, :]
    yj, zj, sj, cj = near[1, p], near[2, p], near[3, p], near[4, p]
    for g in range(GROUPS):
        rows = pl.ds(pl.multiple_of(start + g * 8, 8), 8)
        dx = xj - columns[tile, 0, rows, :]
        dy = yj - columns[tile, 1, rows, :]
        dz = zj - columns[tile, 2, rows, :]
        r2 = dx * dx + dy * dy + dz * dz
        r = r2 * lax.rsqrt(r2)
        x = r2 * r + columns[tile, 3, rows, :] * sj
        inverse = jnp.exp2(lax.log2(x) * (-1.0 / 3.0))
        w = jnp.maximum(CUTOFF - r, 0.0)
        w2 = w * w
        value = (w2 * w2) * (((r + 5.0) * r + 20.0) * r + 50.0) * inverse
        if mask is not None:
            value = jnp.where(mask(g), 0.0, value)
        blocks[tile, slot, rows, :] = value
        sums_t[g] = sums_t[g] + value
        sums_s[g] = sums_s[g] + value * cj


def store(acc, tile, start, sums_s, sums_t):
    for g in range(GROUPS):
        rows = pl.ds(pl.multiple_of(start + g * 8, 8), 8)
        acc[tile, 0, rows, :] = sums_s[g]
        acc[tile, 1, rows, :] = sums_t[g]


def listed(entries, index):
    found = jnp.max(jnp.where(entries == index, 1.0, 0.0), axis=1, keepdims=True)
    return jnp.broadcast_to(jnp.where(found > 0.0, 0.0, FAR), (index.shape[0], ATOMS))


def split(number, by, parts):
    high = sum(jnp.where(number >= by * k, 1, 0) for k in range(1, parts))
    return high, number - by * high


def inner_body(
    received, own, neighbours, chi, eta, gamma,
    blocks, acc, columns, away_outer, table, near, away,
):
    for kind in range(2):
        value = jnp.full((1, ATOMS), gamma[kind], F32)
        table[kind : kind + 1, :] = 1.0 / (value * jnp.sqrt(value))
        table[2 + kind : 3 + kind, :] = jnp.full((1, ATOMS), chi[kind], F32)
        table[4 + kind : 5 + kind, :] = jnp.full((1, ATOMS), eta[kind], F32)
    for b in range(2):
        for c in range(2):
            tile = b * 2 + c
            for field in range(FIELDS):
                row = (c * 2 + b) * FIELDS + field
                values = own[row : row + 1, :]
                if field == 3:
                    values = choose(values, table, 0)
                columns[tile, field] = jnp.broadcast_to(values, (ATOMS, ATOMS)).T
            entries = neighbours[0, b, c : c + 1, :]
            slot = lax.broadcasted_iota(jnp.int32, (18, 27), 0)
            ix, rest = split(slot, 6, 3)
            jy, k = split(rest, 2, 3)
            away[tile] = listed(entries, ix * 16 + (jy + b) * 4 + k + 1)
            slot = lax.broadcasted_iota(jnp.int32, (9, 27), 0)
            ix, jy = split(slot, 3, 3)
            away_outer[tile] = listed(entries, ix * 16 + (jy + b) * 4 + 3 * c)
    for ix, iy, peer, b, step in plane_columns():
        for k in range(2):
            row = (k * 2 + b) * FIELDS
            lines = [received[peer, row + f : row + f + 1, :] for f in range(FIELDS)]
            lines[0] = lines[0] + CELL_EDGE * (ix - 1)
            lines[1] = lines[1] + CELL_EDGE * 2 * step
            place(near, (ix * 4 + iy) * 2 + k, lines, table, 0.0)

    lane = lax.broadcasted_iota(jnp.int32, (8, ATOMS), 1)
    sub = lax.broadcasted_iota(jnp.int32, (8, ATOMS), 0)

    def half_tile(step, carry):
        tile = step // 2
        b, c = tile // 2, tile % 2
        start = (step % 2) * (GROUPS * 8)
        sums_s = [jnp.zeros((8, ATOMS), F32) for _ in range(GROUPS)]
        sums_t = [jnp.zeros((8, ATOMS), F32) for _ in range(GROUPS)]
        for slot, (ix, jy, k) in enumerate(INNER):
            mask = None
            if (ix, jy) == (1, 1):
                first = start + jnp.where(c == k, 0, 2 * ATOMS)
                mask = functools.partial(lambda at, g: lane == sub + (at + g * 8), first)
            p = (ix * 4 + jy + b) * 2 + k
            couple(near, columns, away, tile, start, p, slot, blocks, slot, sums_s, sums_t, mask)
        store(acc, tile, start, sums_s, sums_t)
        return carry

    lax.fori_loop(0, 8, half_tile, 0)


def outer_body(
    below, above, own, columns, away, table, partial,
    blocks, out, head, tail, near, acc,
):
    for ix in range(3):
        for iy in range(4):
            line = (ix * 4 + iy) * FIELDS
            for side, (ghost, lift) in enumerate(((below, -2 * CELL_EDGE), (above, 2 * CELL_EDGE))):
                lines = [ghost[line + f : line + f + 1, :] for f in range(FIELDS)]
                place(near, (ix * 4 + iy) * 2 + side, lines, table, lift)

    def half_tile(step, carry):
        tile = step // 2
        b, c = tile // 2, tile % 2
        start = (step % 2) * (GROUPS * 8)
        rows = [pl.ds(pl.multiple_of(start + g * 8, 8), 8) for g in range(GROUPS)]
        sums_s = [partial[tile, 0, r, :] for r in rows]
        sums_t = [partial[tile, 1, r, :] for r in rows]
        for slot, (ix, jy) in enumerate(OUTER):
            p = (ix * 4 + jy + b) * 2 + c
            couple(near, columns, away, tile, start, p, slot, blocks, slot, sums_s, sums_t, None)
        store(acc, tile, start, sums_s, sums_t)
        return carry

    lax.fori_loop(0, 8, half_tile, 0)
    source = source_rows(own, table)
    next_vector(own, table, source, acc, out, SHIFTS[0], (-SCALE, -SCALE))
    head[...] = out[0:4, :]
    tail[...] = out[4:8, :]


def image_rows(received, inner, outer, near, acc):
    for ix, iy, peer, b, step in plane_columns():
        for iz in range(4):
            for system in range(2):
                row = (iz * 2 + b) * 2 + system
                near[system, (ix * 4 + iy) * 4 + iz] = jnp.broadcast_to(
                    received[peer, row : row + 1, :], (8, ATOMS)
                )
    groups = ATOMS // 8

    def one_tile(tile, carry):
        b, c = tile // 2, tile % 2
        sums_s = [jnp.zeros((8, ATOMS), F32) for _ in range(groups)]
        sums_t = [jnp.zeros((8, ATOMS), F32) for _ in range(groups)]
        places = [((ix * 4 + jy + b) * 4 + k + 1, inner, n) for n, (ix, jy, k) in enumerate(INNER)]
        places += [((ix * 4 + jy + b) * 4 + 3 * c, outer, n) for n, (ix, jy) in enumerate(OUTER)]
        for p, blocks, slot in places:
            vs, vt = near[0, p], near[1, p]
            for g in range(groups):
                value = blocks[tile, slot, g * 8 : g * 8 + 8, :]
                sums_s[g] = sums_s[g] + value * vs
                sums_t[g] = sums_t[g] + value * vt
        for g in range(groups):
            acc[tile, 0, g * 8 : g * 8 + 8, :] = sums_s[g]
            acc[tile, 1, g * 8 : g * 8 + 8, :] = sums_t[g]
        return carry

    lax.fori_loop(0, 4, one_tile, 0)


def next_vector(own, table, vector, acc, out, shift, scales=(SCALE, SCALE)):
    for c in range(2):
        for b in range(2):
            tile = b * 2 + c
            kind = (c * 2 + b) * FIELDS + 3
            shifted = choose(own[kind : kind + 1, :], table, 4) - shift
            for system in range(2):
                line = (c * 2 + b) * 2 + system
                out[line : line + 1, :] = shifted * vector[line : line + 1, :] + scales[
                    system
                ] * row_sums(acc[tile, system])


def second_body(received, inner, outer, own, table, vector, out, head, tail, near, acc):
    image_rows(received, inner, outer, near, acc)
    next_vector(own, table, vector, acc, out, SHIFTS[1])
    head[...] = out[0:4, :]
    tail[...] = out[4:8, :]


def source_rows(own, table):
    rows = []
    for cell in range(4):
        kind = cell * FIELDS + 3
        rows.append(-choose(own[kind : kind + 1, :], table, 2))
        rows.append(jnp.full((1, ATOMS), -1.0, F32))
    return jnp.concatenate(rows, axis=0)


def third_body(received, inner, outer, own, table, w1, w2, out, sums, near, acc, moments):
    image_rows(received, inner, outer, near, acc)
    next_vector(own, table, w2, acc, out, SHIFTS[2])
    v0, v1, v2, v3 = source_rows(own, table), w1[...], w2[...], out[...]
    moments[...] = jnp.zeros((ATOMS, ATOMS), F32)
    pairs = (v0 * v0, v0 * v1, v0 * v2, v1 * v1, v1 * v2, v2 * v2, v2 * v3, v0, v1, v2)
    for k, item in enumerate(pairs):
        moments[2 * k : 2 * k + 2, :] = (item[0:2] + item[2:4]) + (item[4:6] + item[6:8])
    sums[...] = row_sums(moments[...])


def last_body(received, own, table, w1, w2, w3, charges, residuals):
    total = jnp.sum(received[...], axis=0)
    spread = jnp.broadcast_to(total, (ATOMS, ATOMS)).T
    g00, g01, g02, g11, g12, g22, g23, s0, s1, s2 = (spread[2 * k : 2 * k + 2, :] for k in range(10))
    shift0, shift1, shift2 = SHIFTS
    a00 = g01 + shift0 * g00
    a01 = g11 + shift0 * g01
    a02 = g12 + shift0 * g02
    a11 = g12 + shift1 * g11
    a12 = g22 + shift1 * g12
    a22 = g23 + shift2 * g22
    l10 = a01 / a00
    l20 = a02 / a00
    b11 = a11 - l10 * a01
    b12 = a12 - l10 * a02
    b22 = a22 - l20 * a02
    l21 = b12 / b11
    pivot = b22 - l21 * b12
    y1 = g01 - l10 * g00
    y2 = g02 - l20 * g00 - l21 * y1
    c2 = y2 / pivot
    c1 = (y1 - b12 * c2) / b11
    c0 = (g00 - a01 * c1 - a02 * c2) / a00
    level = c0 * s0 + c1 * s1 + c2 * s2
    level = level[0:1] / level[1:2]

    def every(value):
        return jnp.concatenate([value] * 4, axis=0)

    v0, v1, v2, v3 = source_rows(own, table), w1[...], w2[...], w3[...]
    solution_rows = every(c0) * v0 + every(c1) * v1 + every(c2) * v2
    residual_rows = (
        every(1.0 - shift0 * c0) * v0
        - every(c0 + shift1 * c1) * v1
        - every(c1 + shift2 * c2) * v2
        - every(c2) * v3
    )
    for c in range(2):
        for b in range(2):
            row = (c * 2 + b) * 2
            charges[0, b, c : c + 1, :] = 1000.0 * (
                solution_rows[row : row + 1] - level * solution_rows[row + 1 : row + 2]
            )
            for system in range(2):
                residuals[system, 0, b, c : c + 1, :] = residual_rows[row + system : row + system + 1]


def upward(tail):
    count = lax.axis_size(GZ)
    return lax.ppermute(tail, GZ, [(i, (i + 1) % count) for i in range(count)])


def downward(head):
    count = lax.axis_size(GZ)
    return lax.ppermute(head, GZ, [((i + 1) % count, i) for i in range(count)])


def shared(block, axes):
    count = lax.axis_size(axes)
    return lax.all_to_all(
        jnp.broadcast_to(block[None], (count,) + block.shape), axes, 0, 0, tiled=True
    )


def surrounded(own, head, tail):
    return shared(jnp.concatenate([upward(tail), own, downward(head)], axis=0), PLANE)


def per_device(offsets, type_ids, neighbours, type_chi, type_eta, type_gamma):
    smem = pltpu.SMEM
    (own,) = run(
        pack_body,
        [(16, ATOMS)],
        (offsets, type_ids),
        [HBM, HBM],
        [
            VMEM(offsets.shape, F32),
            VMEM(type_ids.shape, jnp.int32),
            pltpu.SemaphoreType.DMA,
            pltpu.SemaphoreType.DMA,
        ],
    )
    received = shared(own, PLANE)
    head, tail = run(faces_body, [(48, ATOMS), (48, ATOMS)], (received,))
    below, above = upward(tail), downward(head)
    products = (4, 2, ATOMS, ATOMS)
    accumulate = VMEM(products, F32)
    inner, partial, columns, away, table = run(
        inner_body,
        [(4, 18, ATOMS, ATOMS), products, (4, FIELDS, ATOMS, ATOMS), (4, 9, ATOMS), (8, ATOMS)],
        (received, own, neighbours, type_chi, type_eta, type_gamma),
        [VMEM, VMEM, VMEM, smem, smem, smem],
        [VMEM((5, 24, 8, ATOMS), F32), VMEM((4, 18, ATOMS), F32)],
    )
    vectors = [(8, ATOMS), (4, ATOMS), (4, ATOMS)]
    outer, w1, head, tail = run(
        outer_body,
        [(4, 9, ATOMS, ATOMS)] + vectors,
        (below, above, own, columns, away, table, partial),
        scratch=[VMEM((5, 24, 8, ATOMS), F32), accumulate],
    )
    near = VMEM((2, 48, 8, ATOMS), F32)
    received = surrounded(w1, head, tail)
    w2, head, tail = run(
        second_body, vectors, (received, inner, outer, own, table, w1), scratch=[near, accumulate]
    )
    received = surrounded(w2, head, tail)
    w3, sums = run(
        third_body,
        [(8, ATOMS), (1, ATOMS)],
        (received, inner, outer, own, table, w1, w2),
        scratch=[near, accumulate, VMEM((ATOMS, ATOMS), F32)],
    )
    half = jnp.sum(shared(sums, GROUP_ONE), axis=0)
    received = shared(half, GROUP_TWO)
    held = [pltpu.with_memory_space_constraint(x, VMEM) for x in (received, own, table, w1, w2, w3)]
    return pl.pallas_call(
        last_body,
        out_shape=(
            jax.ShapeDtypeStruct((1, 2, 2, ATOMS), F32),
            jax.ShapeDtypeStruct((2, 1, 2, 2, ATOMS), F32),
        ),
        in_specs=[pl.BlockSpec(memory_space=VMEM)] * 6,
        out_specs=(pl.BlockSpec(memory_space=VMEM),) * 2,
    )(*held)


def solution(mesh):
    torus = Mesh(
        mesh.devices.reshape(2, 2, mesh.shape["gy"], 8, 8), ("gx_0", "gx_1", "gy", "gz_0", "gz_1")
    )
    in_specs = (
        P(None, GX, "gy", GZ, None),
        P(GX, "gy", GZ, None),
        P(GX, "gy", GZ, None),
        P(),
        P(),
        P(),
    )
    out_specs = (P(GX, "gy", GZ, None), P(None, GX, "gy", GZ, None))
    return jax.shard_map(
        per_device, mesh=torus, in_specs=in_specs, out_specs=out_specs, check_vma=False
    )
```

```python
import functools

import jax
import jax.numpy as jnp
from jax import lax
from jax.experimental import pallas as pl
from jax.experimental.pallas import tpu as pltpu
from jax.sharding import Mesh
from jax.sharding import PartitionSpec as P

GX = ("gx_0", "gx_1")
GZ = ("gz_0", "gz_1")
PLANE = ("gx_0", "gx_1", "gy")
GROUP_ONE = ("gx_0", "gx_1", "gz_1")
GROUP_TWO = ("gy", "gz_0")

CELL_EDGE = 11.0
CUTOFF = 10.0
SCALE = 14.4 * 0.02 / CUTOFF**4
FAR = 1.0e4
ATOMS = 128
GROUPS = ATOMS // 8
FIELDS = 4
SHIFTS = (200.0, 100.0, 20.0)
INNER = tuple((ix, jy, k) for ix in range(3) for jy in range(3) for k in range(2))
OUTER = tuple((ix, jy) for ix in range(3) for jy in range(3))
VMEM = pltpu.VMEM
HBM = pltpu.HBM
F32 = jnp.float32


def run(body, outs, args, spaces=None, scratch=(), far=()):
    spaces = spaces or [VMEM] * len(args)
    held = [
        pltpu.with_memory_space_constraint(x, VMEM if space == VMEM and n not in far else HBM)
        for n, (x, space) in enumerate(zip(args, spaces))
    ]
    return pl.pallas_call(
        body,
        out_shape=tuple(VMEM(shape, F32) for shape in outs),
        in_specs=[pl.BlockSpec(memory_space=space) for space in spaces],
        out_specs=tuple(pl.BlockSpec(memory_space=VMEM) for _ in outs),
        scratch_shapes=list(scratch),
        compiler_params=pltpu.CompilerParams(vmem_limit_bytes=12 * 2**20),
    )(*held)


def pack_body(offsets_far, types_far, own, offsets, type_ids, one, two):
    first = pltpu.make_async_copy(offsets_far, offsets, one)
    second = pltpu.make_async_copy(types_far, type_ids, two)
    first.start()
    second.start()
    first.wait()
    second.wait()
    for c in range(2):
        for b in range(2):
            row = (c * 2 + b) * FIELDS
            for axis in range(3):
                local = 0.0 if axis == 0 else CELL_EDGE * (b if axis == 1 else c)
                own[row + axis : row + axis + 1, :] = offsets[axis, 0, b, c : c + 1, :] + local
            own[row + 3 : row + 4, :] = type_ids[0, b, c : c + 1, :].astype(F32)


def plane_columns():
    first = lax.axis_index("gx_0") * 2 + lax.axis_index("gx_1")
    second = lax.axis_index("gy")
    for ix in range(3):
        for iy in range(4):
            step = -1 if iy == 0 else (1 if iy == 3 else 0)
            peer = ((first + ix + 3) % 4) * 4 + (second + step + 4) % 4
            yield ix, iy, peer, (iy + 1) % 2, step


def faces_body(received, head, tail):
    for ix, iy, peer, b, step in plane_columns():
        for face, c in ((head, 0), (tail, 1)):
            row = (c * 2 + b) * FIELDS
            line = (ix * 4 + iy) * FIELDS
            face[line : line + 1, :] = received[peer, row : row + 1, :] + CELL_EDGE * (ix - 1)
            face[line + 1 : line + 2, :] = received[peer, row + 1 : row + 2, :] + CELL_EDGE * 2 * step
            face[line + 2 : line + 4, :] = received[peer, row + 2 : row + 4, :]


def choose(kinds, table, first):
    return jnp.where(kinds == 0.0, table[first : first + 1, :], table[first + 1 : first + 2, :])


def place(near, index, lines, table, lift):
    x, y, z, kinds = (jnp.broadcast_to(v, (8, ATOMS)) for v in lines)
    near[0, index] = x
    near[1, index] = y
    near[2, index] = z + lift
    near[3, index] = choose(kinds, table, 0)
    near[4, index] = choose(kinds, table, 2)


def row_sums(acc):
    return jnp.sum(acc.T, axis=0, keepdims=True)


def couple(near, columns, away, tile, p, line, blocks, slot, sums_s, sums_t, mask):
    xj = near[0, p] + away[tile, line : line + 1, :]
    yj, zj, sj, cj = near[1, p], near[2, p], near[3, p], near[4, p]
    for g in range(GROUPS):
        rows = pl.ds(g * 8, 8)
        dx = xj - columns[tile, 0, rows, :]
        dy = yj - columns[tile, 1, rows, :]
        dz = zj - columns[tile, 2, rows, :]
        r2 = dx * dx + dy * dy + dz * dz
        r = r2 * lax.rsqrt(r2)
        x = r2 * r + columns[tile, 3, rows, :] * sj
        inverse = jnp.exp2(lax.log2(x) * (-1.0 / 3.0))
        w = jnp.maximum(CUTOFF - r, 0.0)
        w2 = w * w
        value = (w2 * w2) * (((r + 5.0) * r + 20.0) * r + 50.0) * inverse
        if mask is not None:
            value = jnp.where(mask(g), 0.0, value)
        blocks[tile, slot, rows, :] = value
        sums_t[g] = sums_t[g] + value
        sums_s[g] = sums_s[g] + value * cj


def store(acc, tile, sums_s, sums_t):
    for g in range(GROUPS):
        rows = pl.ds(g * 8, 8)
        acc[tile, 0, rows, :] = sums_s[g]
        acc[tile, 1, rows, :] = sums_t[g]


def listed(entries, index):
    found = jnp.max(jnp.where(entries == index, 1.0, 0.0), axis=1, keepdims=True)
    return jnp.broadcast_to(jnp.where(found > 0.0, 0.0, FAR), (index.shape[0], ATOMS))


def split(number, by, parts):
    high = sum(jnp.where(number >= by * k, 1, 0) for k in range(1, parts))
    return high, number - by * high


def inner_body(
    received, own, neighbours, chi, eta, gamma,
    blocks, acc, columns, away_outer, table, near, away,
):
    for kind in range(2):
        value = jnp.full((1, ATOMS), gamma[kind], F32)
        table[kind : kind + 1, :] = 1.0 / (value * jnp.sqrt(value))
        table[2 + kind : 3 + kind, :] = jnp.full((1, ATOMS), chi[kind], F32)
        table[4 + kind : 5 + kind, :] = jnp.full((1, ATOMS), eta[kind], F32)
    for b in range(2):
        for c in range(2):
            tile = b * 2 + c
            for field in range(FIELDS):
                row = (c * 2 + b) * FIELDS + field
                values = own[row : row + 1, :]
                if field == 3:
                    values = choose(values, table, 0)
                columns[tile, field] = jnp.broadcast_to(values, (ATOMS, ATOMS)).T
            entries = neighbours[0, b, c : c + 1, :]
            slot = lax.broadcasted_iota(jnp.int32, (18, 27), 0)
            ix, rest = split(slot, 6, 3)
            jy, k = split(rest, 2, 3)
            away[tile] = listed(entries, ix * 16 + (jy + b) * 4 + k + 1)
            slot = lax.broadcasted_iota(jnp.int32, (9, 27), 0)
            ix, jy = split(slot, 3, 3)
            away_outer[tile] = listed(entries, ix * 16 + (jy + b) * 4 + 3 * c)
    for ix, iy, peer, b, step in plane_columns():
        for k in range(2):
            row = (k * 2 + b) * FIELDS
            lines = [received[peer, row + f : row + f + 1, :] for f in range(FIELDS)]
            lines[0] = lines[0] + CELL_EDGE * (ix - 1)
            lines[1] = lines[1] + CELL_EDGE * 2 * step
            place(near, (ix * 4 + iy) * 2 + k, lines, table, 0.0)

    lane = lax.broadcasted_iota(jnp.int32, (8, ATOMS), 1)
    sub = lax.broadcasted_iota(jnp.int32, (8, ATOMS), 0)

    def one_tile(tile, carry):
        b, c = tile // 2, tile % 2
        sums_s = [jnp.zeros((8, ATOMS), F32) for _ in range(GROUPS)]
        sums_t = [jnp.zeros((8, ATOMS), F32) for _ in range(GROUPS)]
        for slot, (ix, jy, k) in enumerate(INNER):
            mask = None
            if (ix, jy) == (1, 1):
                first = jnp.where(c == k, 0, 2 * ATOMS)
                mask = functools.partial(lambda at, g: lane == sub + (at + g * 8), first)
            p = (ix * 4 + jy + b) * 2 + k
            couple(near, columns, away, tile, p, slot, blocks, slot, sums_s, sums_t, mask)
        store(acc, tile, sums_s, sums_t)
        return carry

    lax.fori_loop(0, 4, one_tile, 0)


def outer_body(
    below, above, own, columns, away, table, partial,
    blocks, out, head, tail, near, acc,
):
    for ix in range(3):
        for iy in range(4):
            line = (ix * 4 + iy) * FIELDS
            for side, (ghost, lift) in enumerate(((below, -2 * CELL_EDGE), (above, 2 * CELL_EDGE))):
                lines = [ghost[line + f : line + f + 1, :] for f in range(FIELDS)]
                place(near, (ix * 4 + iy) * 2 + side, lines, table, lift)

    def one_tile(tile, carry):
        b, c = tile // 2, tile % 2
        rows = [pl.ds(g * 8, 8) for g in range(GROUPS)]
        sums_s = [partial[tile, 0, r, :] for r in rows]
        sums_t = [partial[tile, 1, r, :] for r in rows]
        for slot, (ix, jy) in enumerate(OUTER):
            p = (ix * 4 + jy + b) * 2 + c
            couple(near, columns, away, tile, p, slot, blocks, slot, sums_s, sums_t, None)
        store(acc, tile, sums_s, sums_t)
        return carry

    lax.fori_loop(0, 4, one_tile, 0)
    source = source_rows(own, table)
    next_vector(own, table, source, acc, out, SHIFTS[0], (-SCALE, -SCALE))
    head[...] = out[0:4, :]
    tail[...] = out[4:8, :]


def image_rows(received, inner, outer, near, acc):
    for ix, iy, peer, b, step in plane_columns():
        for iz in range(4):
            for system in range(2):
                row = (iz * 2 + b) * 2 + system
                near[system, (ix * 4 + iy) * 4 + iz] = jnp.broadcast_to(
                    received[peer, row : row + 1, :], (8, ATOMS)
                )
    groups = ATOMS // 8

    def one_tile(tile, carry):
        b, c = tile // 2, tile % 2
        sums_s = [jnp.zeros((8, ATOMS), F32) for _ in range(groups)]
        sums_t = [jnp.zeros((8, ATOMS), F32) for _ in range(groups)]
        places = [((ix * 4 + jy + b) * 4 + k + 1, inner, n) for n, (ix, jy, k) in enumerate(INNER)]
        places += [((ix * 4 + jy + b) * 4 + 3 * c, outer, n) for n, (ix, jy) in enumerate(OUTER)]
        for p, blocks, slot in places:
            vs, vt = near[0, p], near[1, p]
            for g in range(groups):
                value = blocks[tile, slot, g * 8 : g * 8 + 8, :]
                sums_s[g] = sums_s[g] + value * vs
                sums_t[g] = sums_t[g] + value * vt
        for g in range(groups):
            acc[tile, 0, g * 8 : g * 8 + 8, :] = sums_s[g]
            acc[tile, 1, g * 8 : g * 8 + 8, :] = sums_t[g]
        return carry

    lax.fori_loop(0, 4, one_tile, 0)


def next_vector(own, table, vector, acc, out, shift, scales=(SCALE, SCALE)):
    for c in range(2):
        for b in range(2):
            tile = b * 2 + c
            kind = (c * 2 + b) * FIELDS + 3
            shifted = choose(own[kind : kind + 1, :], table, 4) - shift
            for system in range(2):
                line = (c * 2 + b) * 2 + system
                out[line : line + 1, :] = shifted * vector[line : line + 1, :] + scales[
                    system
                ] * row_sums(acc[tile, system])


def second_body(received, inner, outer, own, table, vector, out, head, tail, near, acc):
    image_rows(received, inner, outer, near, acc)
    next_vector(own, table, vector, acc, out, SHIFTS[1])
    head[...] = out[0:4, :]
    tail[...] = out[4:8, :]


def source_rows(own, table):
    rows = []
    for cell in range(4):
        kind = cell * FIELDS + 3
        rows.append(-choose(own[kind : kind + 1, :], table, 2))
        rows.append(jnp.full((1, ATOMS), -1.0, F32))
    return jnp.concatenate(rows, axis=0)


def third_body(received, inner, outer, own, table, w1, w2, out, sums, near, acc, moments):
    image_rows(received, inner, outer, near, acc)
    next_vector(own, table, w2, acc, out, SHIFTS[2])
    v0, v1, v2, v3 = source_rows(own, table), w1[...], w2[...], out[...]
    moments[...] = jnp.zeros((ATOMS, ATOMS), F32)
    pairs = (v0 * v0, v0 * v1, v0 * v2, v1 * v1, v1 * v2, v2 * v2, v2 * v3, v0, v1, v2)
    for k, item in enumerate(pairs):
        moments[2 * k : 2 * k + 2, :] = (item[0:2] + item[2:4]) + (item[4:6] + item[6:8])
    sums[...] = row_sums(moments[...])


def last_body(received, own, table, w1, w2, w3, charges, residuals):
    total = jnp.sum(received[...], axis=0)
    spread = jnp.broadcast_to(total, (ATOMS, ATOMS)).T
    g00, g01, g02, g11, g12, g22, g23, s0, s1, s2 = (spread[2 * k : 2 * k + 2, :] for k in range(10))
    shift0, shift1, shift2 = SHIFTS
    a00 = g01 + shift0 * g00
    a01 = g11 + shift0 * g01
    a02 = g12 + shift0 * g02
    a11 = g12 + shift1 * g11
    a12 = g22 + shift1 * g12
    a22 = g23 + shift2 * g22
    l10 = a01 / a00
    l20 = a02 / a00
    b11 = a11 - l10 * a01
    b12 = a12 - l10 * a02
    b22 = a22 - l20 * a02
    l21 = b12 / b11
    pivot = b22 - l21 * b12
    y1 = g01 - l10 * g00
    y2 = g02 - l20 * g00 - l21 * y1
    c2 = y2 / pivot
    c1 = (y1 - b12 * c2) / b11
    c0 = (g00 - a01 * c1 - a02 * c2) / a00
    level = c0 * s0 + c1 * s1 + c2 * s2
    level = level[0:1] / level[1:2]

    def every(value):
        return jnp.concatenate([value] * 4, axis=0)

    v0, v1, v2, v3 = source_rows(own, table), w1[...], w2[...], w3[...]
    solution_rows = every(c0) * v0 + every(c1) * v1 + every(c2) * v2
    residual_rows = (
        every(1.0 - shift0 * c0) * v0
        - every(c0 + shift1 * c1) * v1
        - every(c1 + shift2 * c2) * v2
        - every(c2) * v3
    )
    for c in range(2):
        for b in range(2):
            row = (c * 2 + b) * 2
            charges[0, b, c : c + 1, :] = 1000.0 * (
                solution_rows[row : row + 1] - level * solution_rows[row + 1 : row + 2]
            )
            for system in range(2):
                residuals[system, 0, b, c : c + 1, :] = residual_rows[row + system : row + system + 1]


def upward(tail):
    count = lax.axis_size(GZ)
    return lax.ppermute(tail, GZ, [(i, (i + 1) % count) for i in range(count)])


def downward(head):
    count = lax.axis_size(GZ)
    return lax.ppermute(head, GZ, [((i + 1) % count, i) for i in range(count)])


def shared(block, axes):
    count = lax.axis_size(axes)
    return lax.all_to_all(
        jnp.broadcast_to(block[None], (count,) + block.shape), axes, 0, 0, tiled=True
    )


def surrounded(own, head, tail):
    return shared(jnp.concatenate([upward(tail), own, downward(head)], axis=0), PLANE)


def per_device(offsets, type_ids, neighbours, type_chi, type_eta, type_gamma):
    smem = pltpu.SMEM
    (own,) = run(
        pack_body,
        [(16, ATOMS)],
        (offsets, type_ids),
        [HBM, HBM],
        [
            VMEM(offsets.shape, F32),
            VMEM(type_ids.shape, jnp.int32),
            pltpu.SemaphoreType.DMA,
            pltpu.SemaphoreType.DMA,
        ],
    )
    received = shared(own, PLANE)
    head, tail = run(faces_body, [(48, ATOMS), (48, ATOMS)], (received,))
    below, above = upward(tail), downward(head)
    products = (4, 2, ATOMS, ATOMS)
    accumulate = VMEM(products, F32)
    inner, partial, columns, away, table = run(
        inner_body,
        [(4, 18, ATOMS, ATOMS), products, (4, FIELDS, ATOMS, ATOMS), (4, 9, ATOMS), (8, ATOMS)],
        (received, own, neighbours, type_chi, type_eta, type_gamma),
        [VMEM, VMEM, VMEM, smem, smem, smem],
        [VMEM((5, 24, 8, ATOMS), F32), VMEM((4, 18, ATOMS), F32)],
        far=(2,),
    )
    vectors = [(8, ATOMS), (4, ATOMS), (4, ATOMS)]
    outer, w1, head, tail = run(
        outer_body,
        [(4, 9, ATOMS, ATOMS)] + vectors,
        (below, above, own, columns, away, table, partial),
        scratch=[VMEM((5, 24, 8, ATOMS), F32), accumulate],
    )
    near = VMEM((2, 48, 8, ATOMS), F32)
    received = surrounded(w1, head, tail)
    w2, head, tail = run(
        second_body, vectors, (received, inner, outer, own, table, w1), scratch=[near, accumulate]
    )
    received = surrounded(w2, head, tail)
    w3, sums = run(
        third_body,
        [(8, ATOMS), (1, ATOMS)],
        (received, inner, outer, own, table, w1, w2),
        scratch=[near, accumulate, VMEM((ATOMS, ATOMS), F32)],
    )
    half = jnp.sum(shared(sums, GROUP_ONE), axis=0)
    received = shared(half, GROUP_TWO)
    held = [pltpu.with_memory_space_constraint(x, VMEM) for x in (received, own, table, w1, w2, w3)]
    return pl.pallas_call(
        last_body,
        out_shape=(
            jax.ShapeDtypeStruct((1, 2, 2, ATOMS), F32),
            jax.ShapeDtypeStruct((2, 1, 2, 2, ATOMS), F32),
        ),
        in_specs=[pl.BlockSpec(memory_space=VMEM)] * 6,
        out_specs=(pl.BlockSpec(memory_space=VMEM),) * 2,
    )(*held)


def solution(mesh):
    torus = Mesh(
        mesh.devices.reshape(2, 2, mesh.shape["gy"], 8, 8), ("gx_0", "gx_1", "gy", "gz_0", "gz_1")
    )
    in_specs = (
        P(None, GX, "gy", GZ, None),
        P(GX, "gy", GZ, None),
        P(GX, "gy", GZ, None),
        P(),
        P(),
        P(),
    )
    out_specs = (P(GX, "gy", GZ, None), P(None, GX, "gy", GZ, None))
    return jax.shard_map(
        per_device, mesh=torus, in_specs=in_specs, out_specs=out_specs, check_vma=False
    )
```

```python
import functools

import jax
import jax.numpy as jnp
from jax import lax
from jax.experimental import pallas as pl
from jax.experimental.pallas import tpu as pltpu
from jax.sharding import Mesh
from jax.sharding import PartitionSpec as P

GX = ("gx_0", "gx_1")
GZ = ("gz_0", "gz_1")
PLANE = ("gx_0", "gx_1", "gy")
GROUP_ONE = ("gx_0", "gx_1", "gz_1")
GROUP_TWO = ("gy", "gz_0")

CELL_EDGE = 11.0
CUTOFF = 10.0
SCALE = 14.4 * 0.02 / CUTOFF**4
FAR = 2.0**20
ATOMS = 128
GROUPS = ATOMS // 8
FIELDS = 4
SHIFTS = (200.0, 100.0, 20.0)
INNER = tuple((ix, jy, k) for ix in range(3) for jy in range(3) for k in range(2))
OUTER = tuple((ix, jy) for ix in range(3) for jy in range(3))
VMEM = pltpu.VMEM
HBM = pltpu.HBM
F32 = jnp.float32
BF16 = jnp.bfloat16
DEPTH = 64
PARTS = ((0, 0), (0, 1), (1, 0), (1, 1), (0, 2), (2, 0), (1, 2), (2, 1))
CENTER = (CELL_EDGE / 2, CELL_EDGE, CELL_EDGE)
CELLS = 24


def run(body, outs, args, spaces=None, scratch=(), far=()):
    spaces = spaces or [VMEM] * len(args)
    held = [
        pltpu.with_memory_space_constraint(x, VMEM if space == VMEM and n not in far else HBM)
        for n, (x, space) in enumerate(zip(args, spaces))
    ]
    return pl.pallas_call(
        body,
        out_shape=tuple(VMEM(shape, F32) for shape in outs),
        in_specs=[pl.BlockSpec(memory_space=space) for space in spaces],
        out_specs=tuple(pl.BlockSpec(memory_space=VMEM) for _ in outs),
        scratch_shapes=list(scratch),
        compiler_params=pltpu.CompilerParams(vmem_limit_bytes=12 * 2**20),
    )(*held)


def pack_body(offsets_far, types_far, own, offsets, type_ids, one, two):
    first = pltpu.make_async_copy(offsets_far, offsets, one)
    second = pltpu.make_async_copy(types_far, type_ids, two)
    first.start()
    second.start()
    first.wait()
    second.wait()
    for c in range(2):
        for b in range(2):
            row = (c * 2 + b) * FIELDS
            for axis in range(3):
                local = 0.0 if axis == 0 else CELL_EDGE * (b if axis == 1 else c)
                own[row + axis : row + axis + 1, :] = offsets[axis, 0, b, c : c + 1, :] + local
            own[row + 3 : row + 4, :] = type_ids[0, b, c : c + 1, :].astype(F32)


def plane_columns():
    first = lax.axis_index("gx_0") * 2 + lax.axis_index("gx_1")
    second = lax.axis_index("gy")
    for ix in range(3):
        for iy in range(4):
            step = -1 if iy == 0 else (1 if iy == 3 else 0)
            peer = ((first + ix + 3) % 4) * 4 + (second + step + 4) % 4
            yield ix, iy, peer, (iy + 1) % 2, step


def faces_body(received, head, tail):
    for ix, iy, peer, b, step in plane_columns():
        for face, c in ((head, 0), (tail, 1)):
            row = (c * 2 + b) * FIELDS
            line = (ix * 4 + iy) * FIELDS
            face[line : line + 1, :] = received[peer, row : row + 1, :] + CELL_EDGE * (ix - 1)
            face[line + 1 : line + 2, :] = received[peer, row + 1 : row + 2, :] + CELL_EDGE * 2 * step
            face[line + 2 : line + 4, :] = received[peer, row + 2 : row + 4, :]


def choose(kinds, table, first):
    return jnp.where(kinds == 0.0, table[first : first + 1, :], table[first + 1 : first + 2, :])


def parts_of(value):
    one = value.astype(BF16).astype(F32)
    rest = value - one
    two = rest.astype(BF16).astype(F32)
    return one, two, (rest - two).astype(BF16).astype(F32)


def fill(coords, near, stack, dense, table, away):
    for n in range(CELLS):
        kinds = jnp.broadcast_to(coords[3, n : n + 1, :], (8, ATOMS))
        near[0, n] = choose(kinds, table, 0)
        near[1, n] = choose(kinds, table, 2)
    stack[...] = jnp.zeros((CELLS * DEPTH, ATOMS), F32)

    def put(row, value):
        stack[pl.ds(row, CELLS, stride=DEPTH), :] = value

    squares = jnp.zeros((CELLS, ATOMS), F32)
    for axis in range(3):
        value = coords[axis]
        squares = squares + value * value
        parts = parts_of(value)
        for m, (_, theirs) in enumerate(PARTS):
            put(8 * axis + m, parts[theirs])
    for m, part in enumerate(parts_of(squares)):
        put(24 + m, jnp.ones((CELLS, ATOMS), F32))
        put(27 + m, part)
    for tile in range(4):
        put(30 + tile, away[tile])
    for n in range(CELLS):
        dense[n] = stack[n * DEPTH : (n + 1) * DEPTH, :].astype(BF16)


def turn(tile, rows, turned):
    turned[...] = jnp.zeros((ATOMS, ATOMS), F32)
    squares = jnp.zeros((1, ATOMS), F32)
    for axis in range(3):
        value = rows[axis] - CENTER[axis]
        squares = squares + value * value
        parts = parts_of(value)
        for m, (ours, _) in enumerate(PARTS):
            turned[8 * axis + m : 8 * axis + m + 1, :] = -2.0 * parts[ours]
    for m, part in enumerate(parts_of(squares)):
        turned[24 + m : 25 + m, :] = part
        turned[27 + m : 28 + m, :] = jnp.ones((1, ATOMS), F32)
    turned[30 + tile : 31 + tile, :] = jnp.ones((1, ATOMS), F32)
    return turned[...].T


def row_sums(acc):
    return jnp.sum(acc.T, axis=0, keepdims=True)


def couple(near, dense, terms, columns, tile, p, blocks, slot, sums_s, sums_t, mask):
    sj, cj = near[0, p], near[1, p]
    squares = jnp.dot(terms, dense[p], preferred_element_type=F32)
    for g in range(GROUPS):
        rows = pl.ds(g * 8, 8)
        r2 = squares[g * 8 : g * 8 + 8]
        r = r2 * lax.rsqrt(r2)
        x = r2 * r + columns[tile, 1, rows, :] * sj
        inverse = jnp.exp2(lax.log2(x) * (-1.0 / 3.0))
        w = jnp.maximum(CUTOFF - r, 0.0)
        w2 = w * w
        value = (w2 * w2) * (((r + 5.0) * r + 20.0) * r + 50.0) * inverse
        if mask is not None:
            value = jnp.where(mask(g), 0.0, value)
        blocks[tile, slot, rows, :] = value
        sums_t[g] = sums_t[g] + value
        sums_s[g] = sums_s[g] + value * cj


def store(acc, tile, sums_s, sums_t):
    for g in range(GROUPS):
        rows = pl.ds(g * 8, 8)
        acc[tile, 0, rows, :] = sums_s[g]
        acc[tile, 1, rows, :] = sums_t[g]


def listed(entries, index):
    found = jnp.max(jnp.where(entries == index, 1.0, 0.0), axis=1, keepdims=True)
    return jnp.broadcast_to(jnp.where(found > 0.0, 0.0, FAR), (index.shape[0], ATOMS))


def inner_body(
    received, own, neighbours, chi, eta, gamma,
    blocks, acc, columns, away_outer, table, near, away, coords, stack, turned, dense,
):
    for kind in range(2):
        value = jnp.full((1, ATOMS), gamma[kind], F32)
        table[kind : kind + 1, :] = 1.0 / (value * jnp.sqrt(value))
        table[2 + kind : 3 + kind, :] = jnp.full((1, ATOMS), chi[kind], F32)
        table[4 + kind : 5 + kind, :] = jnp.full((1, ATOMS), eta[kind], F32)
    cell = lax.broadcasted_iota(jnp.int32, (CELLS, 27), 0)
    side = cell & 1
    for b in range(2):
        for c in range(2):
            tile = b * 2 + c
            row = (c * 2 + b) * FIELDS
            columns[tile, 0] = turn(tile, [own[row + f : row + f + 1, :] for f in range(3)], turned)
            shield = choose(own[row + 3 : row + 4, :], table, 0)
            columns[tile, 1] = jnp.broadcast_to(shield, (ATOMS, ATOMS)).T
            entries = neighbours[0, b, c : c + 1, :]
            away[tile] = listed(entries, (cell - side) * 2 + side + 1)
            away_outer[tile] = listed(entries, (cell - side) * 2 + side * 3)
    for ix, iy, peer, b, step in plane_columns():
        for k in range(2):
            row = (k * 2 + b) * FIELDS
            n = (ix * 4 + iy) * 2 + k
            shift = (CELL_EDGE * (ix - 1), CELL_EDGE * 2 * step, 0.0)
            for axis in range(3):
                line = received[peer, row + axis : row + axis + 1, :]
                coords[axis, n : n + 1, :] = line + (shift[axis] - CENTER[axis])
            coords[3, n : n + 1, :] = received[peer, row + 3 : row + 4, :]
    fill(coords, near, stack, dense, table, away)

    lane = lax.broadcasted_iota(jnp.int32, (8, ATOMS), 1)
    sub = lax.broadcasted_iota(jnp.int32, (8, ATOMS), 0)

    def one_tile(tile, carry):
        b, c = tile // 2, tile % 2
        terms = columns[tile, 0, :, 0:DEPTH].astype(BF16)
        sums_s = [jnp.zeros((8, ATOMS), F32) for _ in range(GROUPS)]
        sums_t = [jnp.zeros((8, ATOMS), F32) for _ in range(GROUPS)]
        for slot, (ix, jy, k) in enumerate(INNER):
            mask = None
            if (ix, jy) == (1, 1):
                first = jnp.where(c == k, 0, 2 * ATOMS)
                mask = functools.partial(lambda at, g: lane == sub + (at + g * 8), first)
            p = (ix * 4 + jy + b) * 2 + k
            couple(near, dense, terms, columns, tile, p, blocks, slot, sums_s, sums_t, mask)
        store(acc, tile, sums_s, sums_t)
        return carry

    lax.fori_loop(0, 4, one_tile, 0)


def outer_body(
    below, above, own, columns, away, table, partial,
    blocks, out, head, tail, near, acc, coords, stack, dense,
):
    for ix in range(3):
        for iy in range(4):
            line = (ix * 4 + iy) * FIELDS
            for side, (ghost, lift) in enumerate(((below, -2 * CELL_EDGE), (above, 2 * CELL_EDGE))):
                n = (ix * 4 + iy) * 2 + side
                for axis in range(3):
                    shift = (lift if axis == 2 else 0.0) - CENTER[axis]
                    coords[axis, n : n + 1, :] = ghost[line + axis : line + axis + 1, :] + shift
                coords[3, n : n + 1, :] = ghost[line + 3 : line + 4, :]
    fill(coords, near, stack, dense, table, away)

    def one_tile(tile, carry):
        b, c = tile // 2, tile % 2
        terms = columns[tile, 0, :, 0:DEPTH].astype(BF16)
        rows = [pl.ds(g * 8, 8) for g in range(GROUPS)]
        sums_s = [partial[tile, 0, r, :] for r in rows]
        sums_t = [partial[tile, 1, r, :] for r in rows]
        for slot, (ix, jy) in enumerate(OUTER):
            p = (ix * 4 + jy + b) * 2 + c
            couple(near, dense, terms, columns, tile, p, blocks, slot, sums_s, sums_t, None)
        store(acc, tile, sums_s, sums_t)
        return carry

    lax.fori_loop(0, 4, one_tile, 0)
    source = source_rows(own, table)
    next_vector(own, table, source, acc, out, SHIFTS[0], (-SCALE, -SCALE))
    head[...] = out[0:4, :]
    tail[...] = out[4:8, :]


def image_rows(received, inner, outer, near, acc):
    for ix, iy, peer, b, step in plane_columns():
        for iz in range(4):
            for system in range(2):
                row = (iz * 2 + b) * 2 + system
                near[system, (ix * 4 + iy) * 4 + iz] = jnp.broadcast_to(
                    received[peer, row : row + 1, :], (8, ATOMS)
                )
    groups = ATOMS // 8

    def one_tile(tile, carry):
        b, c = tile // 2, tile % 2
        sums_s = [jnp.zeros((8, ATOMS), F32) for _ in range(groups)]
        sums_t = [jnp.zeros((8, ATOMS), F32) for _ in range(groups)]
        places = [((ix * 4 + jy + b) * 4 + k + 1, inner, n) for n, (ix, jy, k) in enumerate(INNER)]
        places += [((ix * 4 + jy + b) * 4 + 3 * c, outer, n) for n, (ix, jy) in enumerate(OUTER)]
        for p, blocks, slot in places:
            vs, vt = near[0, p], near[1, p]
            for g in range(groups):
                value = blocks[tile, slot, g * 8 : g * 8 + 8, :]
                sums_s[g] = sums_s[g] + value * vs
                sums_t[g] = sums_t[g] + value * vt
        for g in range(groups):
            acc[tile, 0, g * 8 : g * 8 + 8, :] = sums_s[g]
            acc[tile, 1, g * 8 : g * 8 + 8, :] = sums_t[g]
        return carry

    lax.fori_loop(0, 4, one_tile, 0)


def next_vector(own, table, vector, acc, out, shift, scales=(SCALE, SCALE)):
    for c in range(2):
        for b in range(2):
            tile = b * 2 + c
            kind = (c * 2 + b) * FIELDS + 3
            shifted = choose(own[kind : kind + 1, :], table, 4) - shift
            for system in range(2):
                line = (c * 2 + b) * 2 + system
                out[line : line + 1, :] = shifted * vector[line : line + 1, :] + scales[
                    system
                ] * row_sums(acc[tile, system])


def second_body(received, inner, outer, own, table, vector, out, head, tail, near, acc):
    image_rows(received, inner, outer, near, acc)
    next_vector(own, table, vector, acc, out, SHIFTS[1])
    head[...] = out[0:4, :]
    tail[...] = out[4:8, :]


def source_rows(own, table):
    rows = []
    for cell in range(4):
        kind = cell * FIELDS + 3
        rows.append(-choose(own[kind : kind + 1, :], table, 2))
        rows.append(jnp.full((1, ATOMS), -1.0, F32))
    return jnp.concatenate(rows, axis=0)


def third_body(received, inner, outer, own, table, w1, w2, out, sums, near, acc, moments):
    image_rows(received, inner, outer, near, acc)
    next_vector(own, table, w2, acc, out, SHIFTS[2])
    v0, v1, v2, v3 = source_rows(own, table), w1[...], w2[...], out[...]
    moments[...] = jnp.zeros((ATOMS, ATOMS), F32)
    pairs = (v0 * v0, v0 * v1, v0 * v2, v1 * v1, v1 * v2, v2 * v2, v2 * v3, v0, v1, v2)
    for k, item in enumerate(pairs):
        moments[2 * k : 2 * k + 2, :] = (item[0:2] + item[2:4]) + (item[4:6] + item[6:8])
    sums[...] = row_sums(moments[...])


def last_body(received, own, table, w1, w2, w3, charges, residuals):
    total = jnp.sum(received[...], axis=0)
    spread = jnp.broadcast_to(total, (ATOMS, ATOMS)).T
    g00, g01, g02, g11, g12, g22, g23, s0, s1, s2 = (spread[2 * k : 2 * k + 2, :] for k in range(10))
    shift0, shift1, shift2 = SHIFTS
    a00 = g01 + shift0 * g00
    a01 = g11 + shift0 * g01
    a02 = g12 + shift0 * g02
    a11 = g12 + shift1 * g11
    a12 = g22 + shift1 * g12
    a22 = g23 + shift2 * g22
    l10 = a01 / a00
    l20 = a02 / a00
    b11 = a11 - l10 * a01
    b12 = a12 - l10 * a02
    b22 = a22 - l20 * a02
    l21 = b12 / b11
    pivot = b22 - l21 * b12
    y1 = g01 - l10 * g00
    y2 = g02 - l20 * g00 - l21 * y1
    c2 = y2 / pivot
    c1 = (y1 - b12 * c2) / b11
    c0 = (g00 - a01 * c1 - a02 * c2) / a00
    level = c0 * s0 + c1 * s1 + c2 * s2
    level = level[0:1] / level[1:2]

    def every(value):
        return jnp.concatenate([value] * 4, axis=0)

    v0, v1, v2, v3 = source_rows(own, table), w1[...], w2[...], w3[...]
    solution_rows = every(c0) * v0 + every(c1) * v1 + every(c2) * v2
    residual_rows = (
        every(1.0 - shift0 * c0) * v0
        - every(c0 + shift1 * c1) * v1
        - every(c1 + shift2 * c2) * v2
        - every(c2) * v3
    )
    for c in range(2):
        for b in range(2):
            row = (c * 2 + b) * 2
            charges[0, b, c : c + 1, :] = 1000.0 * (
                solution_rows[row : row + 1] - level * solution_rows[row + 1 : row + 2]
            )
            for system in range(2):
                residuals[system, 0, b, c : c + 1, :] = residual_rows[row + system : row + system + 1]


def upward(tail):
    count = lax.axis_size(GZ)
    return lax.ppermute(tail, GZ, [(i, (i + 1) % count) for i in range(count)])


def downward(head):
    count = lax.axis_size(GZ)
    return lax.ppermute(head, GZ, [((i + 1) % count, i) for i in range(count)])


def shared(block, axes):
    count = lax.axis_size(axes)
    return lax.all_to_all(
        jnp.broadcast_to(block[None], (count,) + block.shape), axes, 0, 0, tiled=True
    )


def surrounded(own, head, tail):
    return shared(jnp.concatenate([upward(tail), own, downward(head)], axis=0), PLANE)


def per_device(offsets, type_ids, neighbours, type_chi, type_eta, type_gamma):
    smem = pltpu.SMEM
    (own,) = run(
        pack_body,
        [(16, ATOMS)],
        (offsets, type_ids),
        [HBM, HBM],
        [
            VMEM(offsets.shape, F32),
            VMEM(type_ids.shape, jnp.int32),
            pltpu.SemaphoreType.DMA,
            pltpu.SemaphoreType.DMA,
        ],
    )
    received = shared(own, PLANE)
    head, tail = run(faces_body, [(48, ATOMS), (48, ATOMS)], (received,))
    below, above = upward(tail), downward(head)
    products = (4, 2, ATOMS, ATOMS)
    accumulate = VMEM(products, F32)
    pairs = VMEM((2, CELLS, 8, ATOMS), F32)
    cells = VMEM((4, CELLS, ATOMS), F32)
    stack = VMEM((CELLS * DEPTH, ATOMS), F32)
    dense = VMEM((CELLS, DEPTH, ATOMS), BF16)
    inner, partial, columns, away, table = run(
        inner_body,
        [(4, 18, ATOMS, ATOMS), products, (4, 2, ATOMS, ATOMS), (4, CELLS, ATOMS), (8, ATOMS)],
        (received, own, neighbours, type_chi, type_eta, type_gamma),
        [VMEM, VMEM, VMEM, smem, smem, smem],
        [pairs, VMEM((4, CELLS, ATOMS), F32), cells, stack, VMEM((ATOMS, ATOMS), F32), dense],
        far=(2,),
    )
    vectors = [(8, ATOMS), (4, ATOMS), (4, ATOMS)]
    outer, w1, head, tail = run(
        outer_body,
        [(4, 9, ATOMS, ATOMS)] + vectors,
        (below, above, own, columns, away, table, partial),
        scratch=[pairs, accumulate, cells, stack, dense],
    )
    near = VMEM((2, 48, 8, ATOMS), F32)
    received = surrounded(w1, head, tail)
    w2, head, tail = run(
        second_body, vectors, (received, inner, outer, own, table, w1), scratch=[near, accumulate]
    )
    received = surrounded(w2, head, tail)
    w3, sums = run(
        third_body,
        [(8, ATOMS), (1, ATOMS)],
        (received, inner, outer, own, table, w1, w2),
        scratch=[near, accumulate, VMEM((ATOMS, ATOMS), F32)],
    )
    half = jnp.sum(shared(sums, GROUP_ONE), axis=0)
    received = shared(half, GROUP_TWO)
    held = [pltpu.with_memory_space_constraint(x, VMEM) for x in (received, own, table, w1, w2, w3)]
    return pl.pallas_call(
        last_body,
        out_shape=(
            jax.ShapeDtypeStruct((1, 2, 2, ATOMS), F32),
            jax.ShapeDtypeStruct((2, 1, 2, 2, ATOMS), F32),
        ),
        in_specs=[pl.BlockSpec(memory_space=VMEM)] * 6,
        out_specs=(pl.BlockSpec(memory_space=VMEM),) * 2,
    )(*held)


def solution(mesh):
    torus = Mesh(
        mesh.devices.reshape(2, 2, mesh.shape["gy"], 8, 8), ("gx_0", "gx_1", "gy", "gz_0", "gz_1")
    )
    in_specs = (
        P(None, GX, "gy", GZ, None),
        P(GX, "gy", GZ, None),
        P(GX, "gy", GZ, None),
        P(),
        P(),
        P(),
    )
    out_specs = (P(GX, "gy", GZ, None), P(None, GX, "gy", GZ, None))
    return jax.shard_map(
        per_device, mesh=torus, in_specs=in_specs, out_specs=out_specs, check_vma=False
    )
```

```python
import functools

import jax
import jax.numpy as jnp
from jax import lax
from jax.experimental import pallas as pl
from jax.experimental.pallas import tpu as pltpu
from jax.sharding import Mesh
from jax.sharding import PartitionSpec as P

GX = ("gx_0", "gx_1")
GZ = ("gz_0", "gz_1")
PLANE = ("gx_0", "gx_1", "gy")
GROUP_ONE = ("gy", "gz_0")
GROUP_TWO = ("gx_0", "gx_1", "gz_1")

CELL_EDGE = 11.0
CUTOFF = 10.0
SCALE = 14.4 * 0.02 / CUTOFF**4
FAR = 1.0e4
ATOMS = 128
GROUPS = ATOMS // 8
FIELDS = 4
SHIFTS = (200.0, 100.0, 20.0)
INNER = tuple((ix, jy, k) for ix in range(3) for jy in range(3) for k in range(2))
OUTER = tuple((ix, jy) for ix in range(3) for jy in range(3))
VMEM = pltpu.VMEM
HBM = pltpu.HBM
F32 = jnp.float32


def run(body, outs, args, spaces=None, scratch=(), far=()):
    spaces = spaces or [VMEM] * len(args)
    held = [
        pltpu.with_memory_space_constraint(x, VMEM if space == VMEM and n not in far else HBM)
        for n, (x, space) in enumerate(zip(args, spaces))
    ]
    return pl.pallas_call(
        body,
        out_shape=tuple(VMEM(shape, F32) for shape in outs),
        in_specs=[pl.BlockSpec(memory_space=space) for space in spaces],
        out_specs=tuple(pl.BlockSpec(memory_space=VMEM) for _ in outs),
        scratch_shapes=list(scratch),
        compiler_params=pltpu.CompilerParams(vmem_limit_bytes=12 * 2**20),
    )(*held)


def pack_body(offsets_far, types_far, own, offsets, type_ids, one, two):
    first = pltpu.make_async_copy(offsets_far, offsets, one)
    second = pltpu.make_async_copy(types_far, type_ids, two)
    first.start()
    second.start()
    first.wait()
    second.wait()
    for c in range(2):
        for b in range(2):
            row = (c * 2 + b) * FIELDS
            for axis in range(3):
                local = 0.0 if axis == 0 else CELL_EDGE * (b if axis == 1 else c)
                own[row + axis : row + axis + 1, :] = offsets[axis, 0, b, c : c + 1, :] + local
            own[row + 3 : row + 4, :] = type_ids[0, b, c : c + 1, :].astype(F32)


def plane_columns():
    first = lax.axis_index("gx_0") * 2 + lax.axis_index("gx_1")
    second = lax.axis_index("gy")
    for ix in range(3):
        for iy in range(4):
            step = -1 if iy == 0 else (1 if iy == 3 else 0)
            peer = ((first + ix + 3) % 4) * 4 + (second + step + 4) % 4
            yield ix, iy, peer, (iy + 1) % 2, step


def faces_body(received, head, tail):
    for ix, iy, peer, b, step in plane_columns():
        for face, c in ((head, 0), (tail, 1)):
            row = (c * 2 + b) * FIELDS
            line = (ix * 4 + iy) * FIELDS
            face[line : line + 1, :] = received[peer, row : row + 1, :] + CELL_EDGE * (ix - 1)
            face[line + 1 : line + 2, :] = received[peer, row + 1 : row + 2, :] + CELL_EDGE * 2 * step
            face[line + 2 : line + 4, :] = received[peer, row + 2 : row + 4, :]


def choose(kinds, table, first):
    return jnp.where(kinds == 0.0, table[first : first + 1, :], table[first + 1 : first + 2, :])


def place(near, index, lines, table, lift):
    x, y, z, kinds = (jnp.broadcast_to(v, (8, ATOMS)) for v in lines)
    near[0, index] = x
    near[1, index] = y
    near[2, index] = z + lift
    near[3, index] = choose(kinds, table, 0)
    near[4, index] = choose(kinds, table, 2)


def row_sums(acc):
    return jnp.sum(acc.T, axis=0, keepdims=True)


def couple(near, columns, away, tile, p, line, blocks, slot, sums_s, sums_t, mask):
    xj = near[0, p] + away[tile, line : line + 1, :]
    yj, zj, sj, cj = near[1, p], near[2, p], near[3, p], near[4, p]
    for g in range(GROUPS):
        rows = pl.ds(g * 8, 8)
        dx = xj - columns[tile, 0, rows, :]
        dy = yj - columns[tile, 1, rows, :]
        dz = zj - columns[tile, 2, rows, :]
        r2 = dx * dx + dy * dy + dz * dz
        r = r2 * lax.rsqrt(r2)
        x = r2 * r + columns[tile, 3, rows, :] * sj
        inverse = jnp.exp2(lax.log2(x) * (-1.0 / 3.0))
        w = jnp.maximum(CUTOFF - r, 0.0)
        w2 = w * w
        value = (w2 * w2) * (((r + 5.0) * r + 20.0) * r + 50.0) * inverse
        if mask is not None:
            value = jnp.where(mask(g), 0.0, value)
        blocks[tile, slot, rows, :] = value
        sums_t[g] = sums_t[g] + value
        sums_s[g] = sums_s[g] + value * cj


def store(acc, tile, sums_s, sums_t):
    for g in range(GROUPS):
        rows = pl.ds(g * 8, 8)
        acc[tile, 0, rows, :] = sums_s[g]
        acc[tile, 1, rows, :] = sums_t[g]


def listed(entries, index):
    found = jnp.max(jnp.where(entries == index, 1.0, 0.0), axis=1, keepdims=True)
    return jnp.broadcast_to(jnp.where(found > 0.0, 0.0, FAR), (index.shape[0], ATOMS))


def split(number, by, parts):
    high = sum(jnp.where(number >= by * k, 1, 0) for k in range(1, parts))
    return high, number - by * high


def inner_body(
    received, own, neighbours, chi, eta, gamma,
    blocks, acc, columns, away_outer, table, near, away,
):
    for kind in range(2):
        value = jnp.full((1, ATOMS), gamma[kind], F32)
        table[kind : kind + 1, :] = 1.0 / (value * jnp.sqrt(value))
        table[2 + kind : 3 + kind, :] = jnp.full((1, ATOMS), chi[kind], F32)
        table[4 + kind : 5 + kind, :] = jnp.full((1, ATOMS), eta[kind], F32)
    for b in range(2):
        for c in range(2):
            tile = b * 2 + c
            for field in range(FIELDS):
                row = (c * 2 + b) * FIELDS + field
                values = own[row : row + 1, :]
                if field == 3:
                    values = choose(values, table, 0)
                columns[tile, field] = jnp.broadcast_to(values, (ATOMS, ATOMS)).T
            entries = neighbours[0, b, c : c + 1, :]
            slot = lax.broadcasted_iota(jnp.int32, (18, 27), 0)
            ix, rest = split(slot, 6, 3)
            jy, k = split(rest, 2, 3)
            away[tile] = listed(entries, ix * 16 + (jy + b) * 4 + k + 1)
            slot = lax.broadcasted_iota(jnp.int32, (9, 27), 0)
            ix, jy = split(slot, 3, 3)
            away_outer[tile] = listed(entries, ix * 16 + (jy + b) * 4 + 3 * c)
    for ix, iy, peer, b, step in plane_columns():
        for k in range(2):
            row = (k * 2 + b) * FIELDS
            lines = [received[peer, row + f : row + f + 1, :] for f in range(FIELDS)]
            lines[0] = lines[0] + CELL_EDGE * (ix - 1)
            lines[1] = lines[1] + CELL_EDGE * 2 * step
            place(near, (ix * 4 + iy) * 2 + k, lines, table, 0.0)

    lane = lax.broadcasted_iota(jnp.int32, (8, ATOMS), 1)
    sub = lax.broadcasted_iota(jnp.int32, (8, ATOMS), 0)

    def one_tile(tile, carry):
        b, c = tile // 2, tile % 2
        sums_s = [jnp.zeros((8, ATOMS), F32) for _ in range(GROUPS)]
        sums_t = [jnp.zeros((8, ATOMS), F32) for _ in range(GROUPS)]
        for slot, (ix, jy, k) in enumerate(INNER):
            mask = None
            if (ix, jy) == (1, 1):
                first = jnp.where(c == k, 0, 2 * ATOMS)
                mask = functools.partial(lambda at, g: lane == sub + (at + g * 8), first)
            p = (ix * 4 + jy + b) * 2 + k
            couple(near, columns, away, tile, p, slot, blocks, slot, sums_s, sums_t, mask)
        store(acc, tile, sums_s, sums_t)
        return carry

    lax.fori_loop(0, 4, one_tile, 0)


def outer_body(
    below, above, own, columns, away, table, partial,
    blocks, out, head, tail, near, acc,
):
    for ix in range(3):
        for iy in range(4):
            line = (ix * 4 + iy) * FIELDS
            for side, (ghost, lift) in enumerate(((below, -2 * CELL_EDGE), (above, 2 * CELL_EDGE))):
                lines = [ghost[line + f : line + f + 1, :] for f in range(FIELDS)]
                place(near, (ix * 4 + iy) * 2 + side, lines, table, lift)

    def one_tile(tile, carry):
        b, c = tile // 2, tile % 2
        rows = [pl.ds(g * 8, 8) for g in range(GROUPS)]
        sums_s = [partial[tile, 0, r, :] for r in rows]
        sums_t = [partial[tile, 1, r, :] for r in rows]
        for slot, (ix, jy) in enumerate(OUTER):
            p = (ix * 4 + jy + b) * 2 + c
            couple(near, columns, away, tile, p, slot, blocks, slot, sums_s, sums_t, None)
        store(acc, tile, sums_s, sums_t)
        return carry

    lax.fori_loop(0, 4, one_tile, 0)
    source = source_rows(own, table)
    next_vector(own, table, source, acc, out, SHIFTS[0], (-SCALE, -SCALE))
    head[...] = out[0:4, :]
    tail[...] = out[4:8, :]


def image_rows(received, inner, outer, near, acc):
    for ix, iy, peer, b, step in plane_columns():
        for iz in range(4):
            for system in range(2):
                row = (iz * 2 + b) * 2 + system
                near[system, (ix * 4 + iy) * 4 + iz] = jnp.broadcast_to(
                    received[peer, row : row + 1, :], (8, ATOMS)
                )
    groups = ATOMS // 8

    def one_tile(tile, carry):
        b, c = tile // 2, tile % 2
        sums_s = [jnp.zeros((8, ATOMS), F32) for _ in range(groups)]
        sums_t = [jnp.zeros((8, ATOMS), F32) for _ in range(groups)]
        places = [((ix * 4 + jy + b) * 4 + k + 1, inner, n) for n, (ix, jy, k) in enumerate(INNER)]
        places += [((ix * 4 + jy + b) * 4 + 3 * c, outer, n) for n, (ix, jy) in enumerate(OUTER)]
        for p, blocks, slot in places:
            vs, vt = near[0, p], near[1, p]
            for g in range(groups):
                value = blocks[tile, slot, g * 8 : g * 8 + 8, :]
                sums_s[g] = sums_s[g] + value * vs
                sums_t[g] = sums_t[g] + value * vt
        for g in range(groups):
            acc[tile, 0, g * 8 : g * 8 + 8, :] = sums_s[g]
            acc[tile, 1, g * 8 : g * 8 + 8, :] = sums_t[g]
        return carry

    lax.fori_loop(0, 4, one_tile, 0)


def next_vector(own, table, vector, acc, out, shift, scales=(SCALE, SCALE)):
    for c in range(2):
        for b in range(2):
            tile = b * 2 + c
            kind = (c * 2 + b) * FIELDS + 3
            shifted = choose(own[kind : kind + 1, :], table, 4) - shift
            for system in range(2):
                line = (c * 2 + b) * 2 + system
                out[line : line + 1, :] = shifted * vector[line : line + 1, :] + scales[
                    system
                ] * row_sums(acc[tile, system])


def second_body(received, inner, outer, own, table, vector, out, head, tail, near, acc):
    image_rows(received, inner, outer, near, acc)
    next_vector(own, table, vector, acc, out, SHIFTS[1])
    head[...] = out[0:4, :]
    tail[...] = out[4:8, :]


def source_rows(own, table):
    rows = []
    for cell in range(4):
        kind = cell * FIELDS + 3
        rows.append(-choose(own[kind : kind + 1, :], table, 2))
        rows.append(jnp.full((1, ATOMS), -1.0, F32))
    return jnp.concatenate(rows, axis=0)


def third_body(received, inner, outer, own, table, w1, w2, out, sums, near, acc, moments):
    image_rows(received, inner, outer, near, acc)
    next_vector(own, table, w2, acc, out, SHIFTS[2])
    v0, v1, v2, v3 = source_rows(own, table), w1[...], w2[...], out[...]
    moments[...] = jnp.zeros((ATOMS, ATOMS), F32)
    pairs = (v0 * v0, v0 * v1, v0 * v2, v1 * v1, v1 * v2, v2 * v2, v2 * v3, v0, v1, v2)
    for k, item in enumerate(pairs):
        moments[2 * k : 2 * k + 2, :] = (item[0:2] + item[2:4]) + (item[4:6] + item[6:8])
    sums[...] = row_sums(moments[...])


def last_body(received, own, table, w1, w2, w3, charges, residuals):
    total = jnp.sum(received[...], axis=0)
    spread = jnp.broadcast_to(total, (ATOMS, ATOMS)).T
    g00, g01, g02, g11, g12, g22, g23, s0, s1, s2 = (spread[2 * k : 2 * k + 2, :] for k in range(10))
    shift0, shift1, shift2 = SHIFTS
    a00 = g01 + shift0 * g00
    a01 = g11 + shift0 * g01
    a02 = g12 + shift0 * g02
    a11 = g12 + shift1 * g11
    a12 = g22 + shift1 * g12
    a22 = g23 + shift2 * g22
    l10 = a01 / a00
    l20 = a02 / a00
    b11 = a11 - l10 * a01
    b12 = a12 - l10 * a02
    b22 = a22 - l20 * a02
    l21 = b12 / b11
    pivot = b22 - l21 * b12
    y1 = g01 - l10 * g00
    y2 = g02 - l20 * g00 - l21 * y1
    c2 = y2 / pivot
    c1 = (y1 - b12 * c2) / b11
    c0 = (g00 - a01 * c1 - a02 * c2) / a00
    level = c0 * s0 + c1 * s1 + c2 * s2
    level = level[0:1] / level[1:2]

    def every(value):
        return jnp.concatenate([value] * 4, axis=0)

    v0, v1, v2, v3 = source_rows(own, table), w1[...], w2[...], w3[...]
    solution_rows = every(c0) * v0 + every(c1) * v1 + every(c2) * v2
    residual_rows = (
        every(1.0 - shift0 * c0) * v0
        - every(c0 + shift1 * c1) * v1
        - every(c1 + shift2 * c2) * v2
        - every(c2) * v3
    )
    for c in range(2):
        for b in range(2):
            row = (c * 2 + b) * 2
            charges[0, b, c : c + 1, :] = 1000.0 * (
                solution_rows[row : row + 1] - level * solution_rows[row + 1 : row + 2]
            )
            for system in range(2):
                residuals[system, 0, b, c : c + 1, :] = residual_rows[row + system : row + system + 1]


def upward(tail):
    count = lax.axis_size(GZ)
    return lax.ppermute(tail, GZ, [(i, (i + 1) % count) for i in range(count)])


def downward(head):
    count = lax.axis_size(GZ)
    return lax.ppermute(head, GZ, [((i + 1) % count, i) for i in range(count)])


def shared(block, axes):
    count = lax.axis_size(axes)
    return lax.all_to_all(
        jnp.broadcast_to(block[None], (count,) + block.shape), axes, 0, 0, tiled=True
    )


def surrounded(own, head, tail):
    return shared(jnp.concatenate([upward(tail), own, downward(head)], axis=0), PLANE)


def per_device(offsets, type_ids, neighbours, type_chi, type_eta, type_gamma):
    smem = pltpu.SMEM
    (own,) = run(
        pack_body,
        [(16, ATOMS)],
        (offsets, type_ids),
        [HBM, HBM],
        [
            VMEM(offsets.shape, F32),
            VMEM(type_ids.shape, jnp.int32),
            pltpu.SemaphoreType.DMA,
            pltpu.SemaphoreType.DMA,
        ],
    )
    received = shared(own, PLANE)
    head, tail = run(faces_body, [(48, ATOMS), (48, ATOMS)], (received,))
    below, above = upward(tail), downward(head)
    products = (4, 2, ATOMS, ATOMS)
    accumulate = VMEM(products, F32)
    inner, partial, columns, away, table = run(
        inner_body,
        [(4, 18, ATOMS, ATOMS), products, (4, FIELDS, ATOMS, ATOMS), (4, 9, ATOMS), (8, ATOMS)],
        (received, own, neighbours, type_chi, type_eta, type_gamma),
        [VMEM, VMEM, VMEM, smem, smem, smem],
        [VMEM((5, 24, 8, ATOMS), F32), VMEM((4, 18, ATOMS), F32)],
        far=(2,),
    )
    vectors = [(8, ATOMS), (4, ATOMS), (4, ATOMS)]
    outer, w1, head, tail = run(
        outer_body,
        [(4, 9, ATOMS, ATOMS)] + vectors,
        (below, above, own, columns, away, table, partial),
        scratch=[VMEM((5, 24, 8, ATOMS), F32), accumulate],
    )
    near = VMEM((2, 48, 8, ATOMS), F32)
    received = surrounded(w1, head, tail)
    w2, head, tail = run(
        second_body, vectors, (received, inner, outer, own, table, w1), scratch=[near, accumulate]
    )
    received = surrounded(w2, head, tail)
    w3, sums = run(
        third_body,
        [(8, ATOMS), (1, ATOMS)],
        (received, inner, outer, own, table, w1, w2),
        scratch=[near, accumulate, VMEM((ATOMS, ATOMS), F32)],
    )
    half = jnp.sum(shared(sums, GROUP_ONE), axis=0)
    received = shared(half, GROUP_TWO)
    held = [pltpu.with_memory_space_constraint(x, VMEM) for x in (received, own, table, w1, w2, w3)]
    return pl.pallas_call(
        last_body,
        out_shape=(
            jax.ShapeDtypeStruct((1, 2, 2, ATOMS), F32),
            jax.ShapeDtypeStruct((2, 1, 2, 2, ATOMS), F32),
        ),
        in_specs=[pl.BlockSpec(memory_space=VMEM)] * 6,
        out_specs=(pl.BlockSpec(memory_space=VMEM),) * 2,
    )(*held)


def solution(mesh):
    torus = Mesh(
        mesh.devices.reshape(2, 2, mesh.shape["gy"], 8, 8), ("gx_0", "gx_1", "gy", "gz_0", "gz_1")
    )
    in_specs = (
        P(None, GX, "gy", GZ, None),
        P(GX, "gy", GZ, None),
        P(GX, "gy", GZ, None),
        P(),
        P(),
        P(),
    )
    out_specs = (P(GX, "gy", GZ, None), P(None, GX, "gy", GZ, None))
    return jax.shard_map(
        per_device, mesh=torus, in_specs=in_specs, out_specs=out_specs, check_vma=False
    )
```
